32 devices in a mesh: depth: 2 (over core), tile: 16 (over z, y, x).
Axes of the slice: x: 2, y: 2, z: 4, core: 2. Of those that a mesh axis runs over, the one named last changes fastest.
Arguments:
- transmission: float32 [2, 4, 1024, 2048], P(None, 'depth', 'tile'), may hold values from -1 to 1, as said below
- probe: float32 [2, 128, 128], replicated, may hold values from -4 to 4
- scan_rows: int32 [128], P('tile'), may hold values from 0 to 896, as said below
- scan_cols: int32 [128], P('tile'), may hold values from 0 to 1920
- tile_counts: int32 [16], replicated, may hold values from 1 to 8, as said below
- diffraction: float32 [128, 128, 128], P('tile'), may hold values from 0 to 2
Outputs:
- object_grad: float32 [2, 4, 1024, 2048], P(None, 'depth', 'tile')
- probe_grad: float32 [2, 128, 128], P(None, 'depth')
The draws below stay inside these ranges and needn't reach their ends.
Inputs may be any that keep to these rules, and one draw needn't show every extreme that they name: `scan_rows`: slot i's row lies within [t * 64 - 128/2, t * 64 + 64 - 128/2) for t = i // 8, clipped to the specimen; both ends of the specimen are reached. `tile_counts`: some strip has all 8 slots filled and some strip only one. `transmission`: every entry has magnitude between 0.8 and 1.
All inputs are finite; a program needn't handle non-finite values.
Results may differ from the reference program's by a relative error of at most 0.0003.
Values sent between devices are 32-bit elements; how exact they have to be, the bound alone decides.
A program may use at most 320 MiB of HBM per device.

```python
import math
import jax
import jax.numpy as jnp
from jax import lax

PROBE = 128
STRIP = 64
COLS = 2048
CAP = 8
SLICES = 4
ROWS = 1024
POSITIONS = 128


def draw_transmission(key, part):
    key_amp, key_phase = jax.random.split(key)
    shape = (SLICES, ROWS, COLS)
    amplitude = 0.85 + 0.15 * jax.random.uniform(key_amp, shape, jnp.float32)
    phase = jax.random.uniform(key_phase, shape, jnp.float32, -1.5, 1.5)
    return jnp.stack([amplitude * jnp.cos(phase), amplitude * jnp.sin(phase)]).astype(jnp.float32)


def draw_scan_rows(key, part):
    index = jnp.arange(POSITIONS, dtype=jnp.int32)
    strip_of = index // CAP
    tiles = POSITIONS // CAP
    offset = jax.random.randint(key, (POSITIONS,), 0, STRIP, dtype=jnp.int32)
    rows = jnp.clip(strip_of * STRIP - PROBE // 2 + offset, 0, ROWS - PROBE)
    rows = jnp.where(index == 0, 0, rows)
    rows = jnp.where(index == (tiles - 1) * CAP, ROWS - PROBE, rows)
    return rows.astype(jnp.int32)


def draw_tile_counts(key, part):
    tiles = POSITIONS // CAP
    key_a, key_b, key_c = jax.random.split(jax.random.fold_in(key, 7), 3)
    counts = jax.random.randint(key_a, (tiles,), 1, CAP // 2 + 1, dtype=jnp.int32)
    full_tile = jax.random.randint(key_b, (), 0, tiles, dtype=jnp.int32)
    single_tile = (full_tile + jax.random.randint(key_c, (), 1, tiles, dtype=jnp.int32)) % tiles
    index = jnp.arange(tiles, dtype=jnp.int32)
    counts = jnp.where(index == full_tile, CAP, jnp.where(index == single_tile, 1, counts))
    return counts.astype(jnp.int32)


def with_ends(values, rng, least, high):
    longest = values.shape.index(max(values.shape))
    spots = []
    for shift in (0, 1):
        where = [jax.random.randint(jax.random.fold_in(rng, axis), (), 0, length) for axis, length in enumerate(values.shape)]
        where[longest] = (where[longest] + shift) % values.shape[longest]
        spots.append(tuple(where))
    return values.at[spots[0]].set(least).at[spots[1]].set(high)


def block_scale(stream_key, dims, cuts, low, largest):
    loudness = 1.0
    for axis_at, shards_of in cuts:
        steps = jax.random.uniform(jax.random.fold_in(jax.random.fold_in(stream_key, 6), axis_at), (shards_of,), jnp.float32, low / len(cuts), largest / len(cuts))
        loudness = loudness * jnp.repeat(jnp.exp(steps), dims[axis_at] // shards_of).reshape((-1,) + (1,) * (len(dims) - 1 - axis_at))
    return loudness


def centred(stream_key, dims, spread, bound, kind=jnp.bfloat16):
    drawn = jax.random.normal(stream_key, dims, jnp.float32) * spread
    return jnp.minimum(jnp.maximum(drawn, -bound), bound).astype(kind)


def setup_inputs(seed: int = 0) -> dict:
    key_list = jax.random.split(jax.random.key(seed), 7)
    return {
        "transmission": draw_transmission(jax.random.fold_in(key_list[6], 71), 0),
        "probe": centred(key_list[1], (2, PROBE, PROBE), 0.7, 4.0, jnp.float32),
        "scan_rows": draw_scan_rows(jax.random.fold_in(key_list[6], 71), 0),
        "scan_cols": with_ends(jax.random.randint(key_list[3], (POSITIONS,), 0, COLS - PROBE + 1), jax.random.fold_in(key_list[3], 1), 0, COLS - PROBE).astype(jnp.int32),
        "tile_counts": draw_tile_counts(jax.random.fold_in(key_list[6], 71), 0),
        "diffraction": jnp.clip(2.0 * jax.random.uniform(key_list[5], (POSITIONS, PROBE, PROBE), jnp.float32) ** block_scale(key_list[5], (POSITIONS, PROBE, PROBE), ((0, 16),), -0.2, 0.2), 0.0, 2.0),
    }


FRESNEL = 0.5
HIGH = lax.Precision.HIGHEST

def dft_tables(size):
    index = jnp.arange(size, dtype=jnp.int32)
    product = index[:, None] * index[None, :] % size
    angle = 2.0 * math.pi / size * product.astype(jnp.float32)
    scale = 1.0 / math.sqrt(size)
    cosine = jnp.cos(angle) * scale
    sine = jnp.sin(angle) * scale
    freq = ((index + size // 2) % size - size // 2).astype(jnp.float32)
    phase = FRESNEL * math.pi / size * (freq[:, None] ** 2 + freq[None, :] ** 2)
    return (cosine, sine, jnp.cos(phase), jnp.sin(phase))

def left_mul(real_m, imag_m, wave):
    wave_re = wave[..., 0, :, :]
    wave_im = wave[..., 1, :, :]

    def prod(m, x):
        return jnp.einsum('ij,...jk->...ik', m, x, precision=HIGH)
    return jnp.stack([prod(real_m, wave_re) - prod(imag_m, wave_im), prod(real_m, wave_im) + prod(imag_m, wave_re)], axis=-3)

def right_mul(wave, real_m, imag_m):
    wave_re = wave[..., 0, :, :]
    wave_im = wave[..., 1, :, :]

    def prod(x, m):
        return jnp.einsum('...ij,jk->...ik', x, m, precision=HIGH)
    return jnp.stack([prod(wave_re, real_m) - prod(wave_im, imag_m), prod(wave_re, imag_m) + prod(wave_im, real_m)], axis=-3)

def transform(wave, cosine, sine, sign):
    imag_m = sign * sine
    return right_mul(left_mul(cosine, imag_m, wave), cosine, imag_m)

def times(first, second):
    a_re, a_im = (first[..., 0, :, :], first[..., 1, :, :])
    b_re, b_im = (second[..., 0, :, :], second[..., 1, :, :])
    return jnp.stack([a_re * b_re - a_im * b_im, a_re * b_im + a_im * b_re], axis=-3)

def conj_times(first, second):
    a_re, a_im = (first[..., 0, :, :], first[..., 1, :, :])
    b_re, b_im = (second[..., 0, :, :], second[..., 1, :, :])
    return jnp.stack([a_re * b_re + a_im * b_im, a_re * b_im - a_im * b_re], axis=-3)

def propagate(wave, tables, adjoint):
    cosine, sine, kern_cos, kern_sin = tables
    spectrum = transform(wave, cosine, sine, -1.0)
    kernel = jnp.stack([kern_cos, kern_sin if adjoint else -kern_sin])
    return transform(times(kernel, spectrum), cosine, sine, 1.0)

def reference(transmission, probe, scan_rows, scan_cols, tile_counts, diffraction):
    tables = dft_tables(PROBE)
    cosine, sine = (tables[0], tables[1])

    def work(args):
        index, grad, probe_grad = args
        row = scan_rows[index]
        col = scan_cols[index]
        start = (jnp.int32(0), jnp.int32(0), row, col)
        patch = lax.dynamic_slice(transmission, start, (2, SLICES, PROBE, PROBE))
        wave = probe
        inputs = []
        for slice_pos in range(SLICES):
            inputs.append(wave)
            wave = propagate(times(patch[:, slice_pos], wave), tables, False)
        far = transform(wave, cosine, sine, -1.0)
        intensity = far[0] ** 2 + far[1] ** 2
        flow = transform((intensity - diffraction[index])[None] * far, cosine, sine, 1.0)
        pieces = [None] * SLICES
        for slice_pos in reversed(range(SLICES)):
            along = propagate(flow, tables, True)
            pieces[slice_pos] = conj_times(inputs[slice_pos], along)
            flow = conj_times(patch[:, slice_pos], along)
        update = jnp.stack(pieces, axis=1)
        current = lax.dynamic_slice(grad, start, (2, SLICES, PROBE, PROBE))
        grad = lax.dynamic_update_slice(grad, current + update, start)
        return (index, grad, probe_grad + flow)

    def skip(args):
        return args

    def one(index, carry):
        grad, probe_grad = carry
        filled = index % CAP < tile_counts[index // CAP]
        _, grad, probe_grad = lax.cond(filled, work, skip, (index, grad, probe_grad))
        return (grad, probe_grad)
    start_grad = jnp.zeros(transmission.shape, jnp.float32)
    start_probe = jnp.zeros(probe.shape, jnp.float32)
    grad, probe_grad = lax.fori_loop(0, POSITIONS, one, (start_grad, start_probe))
    return (grad, probe_grad)
```

```python
import math

import jax
import jax.numpy as jnp
import ml_dtypes
import numpy as np
from jax import lax
from jax.experimental import pallas as pl
from jax.experimental.pallas import tpu as pltpu
from jax.sharding import PartitionSpec as P

FRESNEL = 0.5
LANES = 128


def split_table(table):
    head = table.astype(np.float32).astype(ml_dtypes.bfloat16)
    tail = (table - head.astype(np.float64)).astype(np.float32).astype(ml_dtypes.bfloat16)
    return np.stack([head, tail])


def tables(size):
    index = np.arange(size)
    dft = np.exp(-2j * math.pi / size * (index[:, None] * index[None, :] % size)) / math.sqrt(size)
    freq = (index + size // 2) % size - size // 2
    phase = np.exp(-1j * FRESNEL * math.pi / size * freq.astype(np.float64) ** 2)
    prop = dft.conj() @ (phase[:, None] * dft)
    prop = 0.5 * (prop + prop.T)
    out = []
    for m in (prop, dft):
        right = np.block([[m.real, m.imag], [-m.imag, m.real]])
        out += [split_table(right), split_table(right.T)]
    return out


def halves(x):
    head = x.astype(jnp.bfloat16)
    tail = (x - head.astype(jnp.float32)).astype(jnp.bfloat16)
    return head, tail


def dot(a, b):
    return jnp.dot(a, b, preferred_element_type=jnp.float32)


def two_sided(re, im, right, left, slots, size):
    head, tail = halves(jnp.concatenate([re, im], axis=1))
    y = dot(head, right[0]) + dot(tail, right[0]) + dot(head, right[1])
    z = jnp.concatenate(
        [
            jnp.concatenate(
                [y[j * size : (j + 1) * size, :size], y[j * size : (j + 1) * size, size:]], axis=0
            )
            for j in range(slots)
        ],
        axis=1,
    )
    head, tail = halves(z)
    y = dot(left[0], head) + dot(left[0], tail) + dot(left[1], head)
    out_re = [y[:size, j * size : (j + 1) * size] for j in range(slots)]
    out_im = [y[size:, j * size : (j + 1) * size] for j in range(slots)]
    return jnp.concatenate(out_re, axis=0), jnp.concatenate(out_im, axis=0)


def gather_kernel(pos, trans, *outs):
    depth = pos[0, 0]
    blocks = trans.shape[2] // LANES
    shape = (trans.shape[0], trans.shape[1], LANES)
    lane = lax.broadcasted_iota(jnp.int32, shape, 2)
    for which in range(3):
        for rel in range(2):
            out = outs[2 * which + rel]

            def one(j, carry, which=which, rel=rel, out=out):
                slot = 2 * j + (depth if rel == 0 else 1 - depth)
                col = pos[2 + 2 * which, slot]
                block = col // LANES
                after = jnp.minimum(block + 1, blocks - 1)
                x = trans[:, :, pl.ds(pl.multiple_of(block * LANES, LANES), LANES)]
                y = trans[:, :, pl.ds(pl.multiple_of(after * LANES, LANES), LANES)]
                out[j] = jnp.where(lane >= col - block * LANES, x, y)
                return carry

            lax.fori_loop(0, out.shape[0], one, 0)


def wave_kernel(
    pos, probe, diff, keep_rim, keep_own, got_rim, got_own, a_right, a_left, f_right, f_left,
    rim_keep, own_keep, rim_give, own_give, probe_out, patch, psi,
):
    depth = pos[0, 0]
    filled = pos[0, 1]
    rounds, _, half, size = keep_rim.shape
    group = keep_rim.shape[1] // 2
    slices = 2 * group

    def slot_of(j):
        return 2 * j + depth

    def rows(j):
        return slice(j * size, (j + 1) * size)

    def shift_of(j):
        return pos[1, slot_of(j)], pos[2, slot_of(j)] % LANES

    for j in range(rounds):
        down, across = shift_of(j)
        for part in range(2):
            rolled = pltpu.roll(pltpu.roll(probe[part], down, 0), across, 1)
            psi[0, part, rows(j), :] = rolled
            for s in range(slices):
                a = part * group + s % group
                mine = depth == s // group
                patch[s, part, j * size : j * size + half, :] = jnp.where(
                    mine, keep_rim[j, a], got_rim[j, a]
                )
                patch[s, part, j * size + half : (j + 1) * size, :] = jnp.where(
                    mine, keep_own[j, a], got_own[j, a]
                )

    def times(a, b):
        return a[0] * b[0] - a[1] * b[1], a[0] * b[1] + a[1] * b[0]

    def load(ref, s):
        return ref[s, 0], ref[s, 1]

    def apply(wave, right, left):
        return two_sided(wave[0], wave[1], right, left, rounds, size)

    for s in range(slices - 1):
        wave = apply(times(load(patch, s), load(psi, s)), a_right, a_left)
        psi[s + 1, 0] = wave[0]
        psi[s + 1, 1] = wave[1]
    far = apply(times(load(patch, slices - 1), load(psi, slices - 1)), f_right, f_left)
    measured = jnp.concatenate([diff[slot_of(j)] for j in range(rounds)], axis=0)
    misfit = far[0] * far[0] + far[1] * far[1] - measured
    back = (misfit * far[0], -(misfit * far[1]))
    for s in reversed(range(slices)):
        if s == slices - 1:
            along = apply(back, f_right, f_left)
        else:
            along = apply(back, a_right, a_left)
        term = times(load(psi, s), along)
        term = (term[0], -term[1])
        back = times(load(patch, s), along)
        mine = depth == s // group

        def store(rim, own, term=term, s=s):
            for j in range(rounds):
                on = slot_of(j) < filled
                for part in range(2):
                    a = part * group + s % group
                    value = jnp.where(on, term[part][rows(j)], 0.0)
                    rim[j, a] = value[:half]
                    own[j, a] = value[half:]

        @pl.when(mine)
        def _(store=store):
            store(rim_keep, own_keep)

        @pl.when(jnp.logical_not(mine))
        def _(store=store):
            store(rim_give, own_give)

    for part in range(2):
        total = jnp.zeros((size, size), jnp.float32)
        for j in range(rounds):
            down, across = shift_of(j)
            value = jnp.where(slot_of(j) < filled, back[part][rows(j)], 0.0)
            value = pltpu.roll(value, lax.rem(size - down, size), 0)
            total = total + pltpu.roll(value, lax.rem(size - across, size), 1)
        probe_out[part] = total if part == 0 else -total


def scatter_kernel(pos, own_k, own_g, near_k, near_g, far_k, far_g, out):
    depth = pos[0, 0]
    odd = pos[0, 2]
    blocks = out.shape[2] // LANES
    shape = (out.shape[0], out.shape[1], LANES)
    lane = lax.broadcasted_iota(jnp.int32, shape, 2)
    row = lax.broadcasted_iota(jnp.int32, shape, 1)
    out[...] = jnp.zeros_like(out)
    for index, ref in enumerate((own_k, own_g, near_k, near_g, far_k, far_g)):
        which, rel = index // 2, index % 2

        def one(j, carry, which=which, rel=rel, ref=ref):
            slot = 2 * j + (depth if rel == 0 else 1 - depth)
            value = ref[j]
            col = pos[2 + 2 * which, slot]
            if which:
                under = odd if which == 1 else 1 - odd
                start = pos[1 + 2 * which, slot]
                low = jnp.where(under == 1, 0, start)
                high = jnp.where(under == 1, start, shape[1])
                value = jnp.where((row >= low) & (row < high), value, 0.0)
            block = col // LANES
            after = jnp.minimum(block + 1, blocks - 1)
            inside = lane >= col - block * LANES
            at = pl.ds(pl.multiple_of(block * LANES, LANES), LANES)
            out[:, :, at] = out[:, :, at] + jnp.where(inside, value, 0.0)
            at = pl.ds(pl.multiple_of(after * LANES, LANES), LANES)
            out[:, :, at] = out[:, :, at] + jnp.where(inside, 0.0, value)
            return carry

        lax.fori_loop(0, ref.shape[0], one, 0)


SMEM = pl.BlockSpec(memory_space=pltpu.SMEM)
VMEM = pl.BlockSpec(memory_space=pltpu.VMEM)
PARAMS = pltpu.CompilerParams(vmem_limit_bytes=48 * 1024 * 1024)


def shards(transmission, probe, scan_rows, scan_cols, tile_counts, diffraction):
    size = probe.shape[-1]
    half = size // 2
    group, strip, cols = transmission.shape[1:]
    rounds = scan_rows.shape[0] // 2
    tiles = lax.axis_size("tile")
    depth = lax.axis_index("depth")
    tile = lax.axis_index("tile")
    odd = tile % 2
    f32 = jnp.float32

    beside = [(c, c ^ 1) for c in range(tiles)]
    across = [(c, c + 1 if c % 2 else c - 1) for c in range(1, tiles - 1)]
    hop = [(c, c + 2 if c % 2 else c - 2) for c in range(tiles)]
    hop = [(a, b) for a, b in hop if 0 <= b < tiles]
    hop_back = [(b, a) for a, b in hop]
    swap = [(0, 1), (1, 0)]

    start = scan_rows - (tile * strip - half)
    place = jnp.stack([start, scan_cols]).astype(jnp.int32)
    place_near = lax.ppermute(place, "tile", beside)
    place_far = lax.ppermute(place, "tile", across)
    head = jnp.zeros((1, scan_rows.shape[0]), jnp.int32)
    head = head.at[0, 0].set(depth).at[0, 1].set(tile_counts[tile]).at[0, 2].set(odd)
    pos = jnp.concatenate([head, place, place_near, place_far], axis=0)

    flat = transmission.reshape(2 * group, strip, cols)
    piece = jax.ShapeDtypeStruct((rounds, 2 * group, strip, LANES), f32)
    own_k, own_g, near_k, near_g, far_k, far_g = pl.pallas_call(
        gather_kernel,
        out_shape=[piece] * 6,
        in_specs=[SMEM, VMEM],
        out_specs=[VMEM] * 6,
        compiler_params=PARAMS,
        name="gather",
    )(pos, flat)

    near_start = place_near[0].reshape(rounds, 2)

    def rim_of(near, far, parity):
        begin = lax.dynamic_index_in_dim(near_start, parity, 1, keepdims=False)
        row = lax.broadcasted_iota(jnp.int32, near.shape, 2)
        above = row >= begin[:, None, None, None]
        return jnp.where(above == (odd == 0), near, far)

    hop_g = lax.ppermute(far_g, "tile", hop)
    hop_k = lax.ppermute(far_k, "tile", hop)
    own_got = lax.ppermute(own_g, "depth", swap)
    rim_g = lax.ppermute(rim_of(near_g, hop_g, 1 - depth), "tile", beside)
    rim_k = lax.ppermute(rim_of(near_k, hop_k, depth), "tile", beside)
    rim_got = lax.ppermute(rim_g, "depth", swap)

    tabs = [jnp.asarray(t) for t in tables(size)]
    waves = (2 * group, 2, rounds * size, size)
    rim_keep, own_keep, rim_give, own_give, probe_part = pl.pallas_call(
        wave_kernel,
        out_shape=[piece] * 4 + [jax.ShapeDtypeStruct(probe.shape, f32)],
        in_specs=[SMEM] + [VMEM] * 10,
        out_specs=[VMEM] * 5,
        scratch_shapes=[pltpu.VMEM(waves, f32), pltpu.VMEM(waves, f32)],
        compiler_params=PARAMS,
        name="waves",
    )(pos, probe, diffraction, rim_k, own_k, rim_got, own_got, *tabs)

    rim_back = lax.ppermute(rim_give, "depth", swap)
    own_back = lax.ppermute(own_give, "depth", swap)
    near_k = lax.ppermute(rim_keep, "tile", beside)
    near_g = lax.ppermute(rim_back, "tile", beside)
    far_k = lax.ppermute(near_k, "tile", hop_back)
    far_g = lax.ppermute(near_g, "tile", hop_back)
    probe_rows = lax.psum_scatter(probe_part, "depth", scatter_dimension=1, tiled=True)
    probe_grad = lax.psum(probe_rows, "tile")

    grads = pl.pallas_call(
        scatter_kernel,
        out_shape=jax.ShapeDtypeStruct(flat.shape, f32),
        in_specs=[SMEM] + [VMEM] * 6,
        out_specs=VMEM,
        compiler_params=PARAMS,
        name="scatter",
    )(pos, own_keep, own_back, near_k, near_g, far_k, far_g)
    return (grads.reshape(transmission.shape), probe_grad)


def solution(mesh):
    placed = (P(None, "depth", "tile", None), P(), P("tile"), P("tile"), P(), P("tile", None, None))
    return jax.shard_map(
        shards,
        mesh=mesh,
        in_specs=placed,
        out_specs=(P(None, "depth", "tile", None), P(None, "depth", None)),
        check_vma=False,
    )
```

```python
import math

import jax
import jax.numpy as jnp
import ml_dtypes
import numpy as np
from jax import lax
from jax.experimental import pallas as pl
from jax.experimental.pallas import tpu as pltpu
from jax.sharding import PartitionSpec as P

FRESNEL = 0.5
LANES = 128


def split_table(table):
    head = table.astype(np.float32).astype(ml_dtypes.bfloat16)
    tail = (table - head.astype(np.float64)).astype(np.float32).astype(ml_dtypes.bfloat16)
    return np.stack([head, tail])


def tables(size):
    index = np.arange(size)
    dft = np.exp(-2j * math.pi / size * (index[:, None] * index[None, :] % size)) / math.sqrt(size)
    freq = (index + size // 2) % size - size // 2
    phase = np.exp(-1j * FRESNEL * math.pi / size * freq.astype(np.float64) ** 2)
    prop = dft.conj() @ (phase[:, None] * dft)
    prop = 0.5 * (prop + prop.T)
    out = []
    for m in (prop, dft):
        right = np.block([[m.real, m.imag], [-m.imag, m.real]])
        out += [split_table(right), split_table(right.T)]
    return out


def halves(x):
    head = x.astype(jnp.bfloat16)
    tail = (x - head.astype(jnp.float32)).astype(jnp.bfloat16)
    return head, tail


def dot(a, b):
    return jnp.dot(a, b, preferred_element_type=jnp.float32)


def two_sided(re, im, right, left, slots, size):
    head, tail = halves(jnp.concatenate([re, im], axis=1))
    y = dot(head, right[0]) + dot(tail, right[0]) + dot(head, right[1])
    z = jnp.concatenate(
        [
            jnp.concatenate(
                [y[j * size : (j + 1) * size, :size], y[j * size : (j + 1) * size, size:]], axis=0
            )
            for j in range(slots)
        ],
        axis=1,
    )
    head, tail = halves(z)
    y = dot(left[0], head) + dot(left[0], tail) + dot(left[1], head)
    out_re = [y[:size, j * size : (j + 1) * size] for j in range(slots)]
    out_im = [y[size:, j * size : (j + 1) * size] for j in range(slots)]
    return jnp.concatenate(out_re, axis=0), jnp.concatenate(out_im, axis=0)


def axis_places():
    depth = lax.axis_index("depth")
    tile = lax.axis_index("tile")
    return depth, tile, lax.rem(tile, 2)


def gather_kernel(own_cols, near_place, far_place, trans, *outs):
    depth, _, _ = axis_places()
    blocks = trans.shape[2] // LANES
    shape = (trans.shape[0], trans.shape[1], LANES)
    lane = lax.broadcasted_iota(jnp.int32, shape, 2)
    for which in range(3):
        for rel in range(2):
            out = outs[2 * which + rel]

            def one(j, carry, which=which, rel=rel, out=out):
                slot = 2 * j + (depth if rel == 0 else 1 - depth)
                col = own_cols[slot] if which == 0 else (near_place, far_place)[which - 1][1, slot]
                block = col // LANES
                after = jnp.minimum(block + 1, blocks - 1)
                x = trans[:, :, pl.ds(pl.multiple_of(block * LANES, LANES), LANES)]
                y = trans[:, :, pl.ds(pl.multiple_of(after * LANES, LANES), LANES)]
                out[j] = jnp.where(lane >= col - block * LANES, x, y)
                return carry

            lax.fori_loop(0, out.shape[0], one, 0)


def wave_kernel(
    own_rows, own_cols, counts, probe, diff, keep_rim, keep_own, got_rim, got_own, a_right, a_left, f_right, f_left,
    rim_keep, own_keep, rim_give, own_give, probe_out, patch, psi,
):
    depth, tile, _ = axis_places()
    filled = counts[tile]
    rounds, _, half, size = keep_rim.shape
    group = keep_rim.shape[1] // 2
    slices = 2 * group

    def slot_of(j):
        return 2 * j + depth

    def rows(j):
        return slice(j * size, (j + 1) * size)

    def shift_of(j):
        slot = slot_of(j)
        return own_rows[slot] - (tile * half - half), lax.rem(own_cols[slot], LANES)

    for j in range(rounds):
        down, across = shift_of(j)
        for part in range(2):
            rolled = pltpu.roll(pltpu.roll(probe[part], down, 0), across, 1)
            psi[0, part, rows(j), :] = rolled
            for s in range(slices):
                a = part * group + s % group
                mine = depth == s // group
                patch[s, part, j * size : j * size + half, :] = jnp.where(
                    mine, keep_rim[j, a], got_rim[j, a]
                )
                patch[s, part, j * size + half : (j + 1) * size, :] = jnp.where(
                    mine, keep_own[j, a], got_own[j, a]
                )

    def times(a, b):
        return a[0] * b[0] - a[1] * b[1], a[0] * b[1] + a[1] * b[0]

    def load(ref, s):
        return ref[s, 0], ref[s, 1]

    def apply(wave, right, left):
        return two_sided(wave[0], wave[1], right, left, rounds, size)

    for s in range(slices - 1):
        wave = apply(times(load(patch, s), load(psi, s)), a_right, a_left)
        psi[s + 1, 0] = wave[0]
        psi[s + 1, 1] = wave[1]
    far = apply(times(load(patch, slices - 1), load(psi, slices - 1)), f_right, f_left)
    measured = jnp.concatenate([diff[slot_of(j)] for j in range(rounds)], axis=0)
    misfit = far[0] * far[0] + far[1] * far[1] - measured
    back = (misfit * far[0], -(misfit * far[1]))
    for s in reversed(range(slices)):
        if s == slices - 1:
            along = apply(back, f_right, f_left)
        else:
            along = apply(back, a_right, a_left)
        term = times(load(psi, s), along)
        term = (term[0], -term[1])
        back = times(load(patch, s), along)
        mine = depth == s // group

        def store(rim, own, term=term, s=s):
            for j in range(rounds):
                on = slot_of(j) < filled
                for part in range(2):
                    a = part * group + s % group
                    value = jnp.where(on, term[part][rows(j)], 0.0)
                    rim[j, a] = value[:half]
                    own[j, a] = value[half:]

        @pl.when(mine)
        def _(store=store):
            store(rim_keep, own_keep)

        @pl.when(jnp.logical_not(mine))
        def _(store=store):
            store(rim_give, own_give)

    for part in range(2):
        total = jnp.zeros((size, size), jnp.float32)
        for j in range(rounds):
            down, across = shift_of(j)
            value = jnp.where(slot_of(j) < filled, back[part][rows(j)], 0.0)
            value = pltpu.roll(value, lax.rem(size - down, size), 0)
            total = total + pltpu.roll(value, lax.rem(size - across, size), 1)
        probe_out[part] = total if part == 0 else -total


def scatter_kernel(own_cols, near_place, far_place, own_k, own_g, near_k, near_g, far_k, far_g, out):
    depth, tile, odd = axis_places()
    blocks = out.shape[2] // LANES
    shape = (out.shape[0], out.shape[1], LANES)
    lane = lax.broadcasted_iota(jnp.int32, shape, 2)
    row = lax.broadcasted_iota(jnp.int32, shape, 1)
    out[...] = jnp.zeros_like(out)
    for index, ref in enumerate((own_k, own_g, near_k, near_g, far_k, far_g)):
        which, rel = index // 2, index % 2

        def one(j, carry, which=which, rel=rel, ref=ref):
            slot = 2 * j + (depth if rel == 0 else 1 - depth)
            value = ref[j]
            col = own_cols[slot] if which == 0 else (near_place, far_place)[which - 1][1, slot]
            if which:
                under = odd if which == 1 else 1 - odd
                place = (near_place, far_place)[which - 1]
                owner = tile + (1 - 2 * odd if which == 1 else 2 * odd - 1)
                start = place[0, slot] - (owner - 1) * shape[1]
                low = jnp.where(under == 1, 0, start)
                high = jnp.where(under == 1, start, shape[1])
                value = jnp.where((row >= low) & (row < high), value, 0.0)
            block = col // LANES
            after = jnp.minimum(block + 1, blocks - 1)
            inside = lane >= col - block * LANES
            at = pl.ds(pl.multiple_of(block * LANES, LANES), LANES)
            out[:, :, at] = out[:, :, at] + jnp.where(inside, value, 0.0)
            at = pl.ds(pl.multiple_of(after * LANES, LANES), LANES)
            out[:, :, at] = out[:, :, at] + jnp.where(inside, 0.0, value)
            return carry

        lax.fori_loop(0, ref.shape[0], one, 0)


SMEM = pl.BlockSpec(memory_space=pltpu.SMEM)
VMEM = pl.BlockSpec(memory_space=pltpu.VMEM)
PARAMS = pltpu.CompilerParams(vmem_limit_bytes=48 * 1024 * 1024)


def shards(transmission, probe, scan_rows, scan_cols, tile_counts, diffraction):
    size = probe.shape[-1]
    half = size // 2
    group, strip, cols = transmission.shape[1:]
    rounds = scan_rows.shape[0] // 2
    tiles = lax.axis_size("tile")
    depth = lax.axis_index("depth")
    tile = lax.axis_index("tile")
    odd = tile % 2
    f32 = jnp.float32

    beside = [(c, c ^ 1) for c in range(tiles)]
    across = [(c, c + 1 if c % 2 else c - 1) for c in range(1, tiles - 1)]
    hop = [(c, c + 2 if c % 2 else c - 2) for c in range(tiles)]
    hop = [(a, b) for a, b in hop if 0 <= b < tiles]
    hop_back = [(b, a) for a, b in hop]
    swap = [(0, 1), (1, 0)]

    place = jnp.stack([scan_rows, scan_cols])
    place_near = lax.ppermute(place, "tile", beside)
    place_far = lax.ppermute(place, "tile", across)

    flat = transmission.reshape(2 * group, strip, cols)
    piece = jax.ShapeDtypeStruct((rounds, 2 * group, strip, LANES), f32)
    own_k, own_g, near_k, near_g, far_k, far_g = pl.pallas_call(
        gather_kernel,
        out_shape=[piece] * 6,
        in_specs=[SMEM] * 3 + [VMEM],
        out_specs=[VMEM] * 6,
        compiler_params=PARAMS,
        name="gather",
    )(scan_cols, place_near, place_far, flat)

    near_tile = tile + 1 - 2 * odd
    near_start = (place_near[0] - (near_tile - 1) * strip).reshape(rounds, 2)

    def rim_of(near, far, parity):
        begin = lax.dynamic_index_in_dim(near_start, parity, 1, keepdims=False)
        row = lax.broadcasted_iota(jnp.int32, near.shape, 2)
        above = row >= begin[:, None, None, None]
        return jnp.where(above == (odd == 0), near, far)

    hop_g = lax.ppermute(far_g, "tile", hop)
    hop_k = lax.ppermute(far_k, "tile", hop)
    own_got = lax.ppermute(own_g, "depth", swap)
    rim_g = lax.ppermute(rim_of(near_g, hop_g, 1 - depth), "tile", beside)
    rim_k = lax.ppermute(rim_of(near_k, hop_k, depth), "tile", beside)
    rim_got = lax.ppermute(rim_g, "depth", swap)

    tabs = [jnp.asarray(t) for t in tables(size)]
    waves = (2 * group, 2, rounds * size, size)
    rim_keep, own_keep, rim_give, own_give, probe_part = pl.pallas_call(
        wave_kernel,
        out_shape=[piece] * 4 + [jax.ShapeDtypeStruct(probe.shape, f32)],
        in_specs=[SMEM] * 3 + [VMEM] * 10,
        out_specs=[VMEM] * 5,
        scratch_shapes=[pltpu.VMEM(waves, f32), pltpu.VMEM(waves, f32)],
        compiler_params=PARAMS,
        name="waves",
    )(scan_rows, scan_cols, tile_counts, probe, diffraction, rim_k, own_k, rim_got, own_got, *tabs)

    rim_back = lax.ppermute(rim_give, "depth", swap)
    own_back = lax.ppermute(own_give, "depth", swap)
    near_k = lax.ppermute(rim_keep, "tile", beside)
    near_g = lax.ppermute(rim_back, "tile", beside)
    far_k = lax.ppermute(near_k, "tile", hop_back)
    far_g = lax.ppermute(near_g, "tile", hop_back)
    probe_halves = probe_part.reshape(2, 2, half, size)
    kept = lax.dynamic_index_in_dim(probe_halves, depth, 1, keepdims=False)
    given = lax.dynamic_index_in_dim(probe_halves, 1 - depth, 1, keepdims=False)
    probe_grad = kept + lax.ppermute(given, "depth", swap)
    step = 1
    while step < tiles:
        pairs = [(c, c ^ step) for c in range(tiles)]
        probe_grad = probe_grad + lax.ppermute(probe_grad, "tile", pairs)
        step *= 2

    grads = pl.pallas_call(
        scatter_kernel,
        out_shape=jax.ShapeDtypeStruct(flat.shape, f32),
        in_specs=[SMEM] * 3 + [VMEM] * 6,
        out_specs=VMEM,
        compiler_params=PARAMS,
        name="scatter",
    )(scan_cols, place_near, place_far, own_keep, own_back, near_k, near_g, far_k, far_g)
    return (grads.reshape(transmission.shape), probe_grad)


def solution(mesh):
    placed = (P(None, "depth", "tile", None), P(), P("tile"), P("tile"), P(), P("tile", None, None))
    return jax.shard_map(
        shards,
        mesh=mesh,
        in_specs=placed,
        out_specs=(P(None, "depth", "tile", None), P(None, "depth", None)),
        check_vma=False,
    )
```

```python
import math

import jax
import jax.numpy as jnp
import ml_dtypes
import numpy as np
from jax import lax
from jax.experimental import pallas as pl
from jax.experimental.pallas import tpu as pltpu
from jax.sharding import PartitionSpec as P

FRESNEL = 0.5
LANES = 128


def split_table(table):
    head = table.astype(np.float32).astype(ml_dtypes.bfloat16)
    tail = (table - head.astype(np.float64)).astype(np.float32).astype(ml_dtypes.bfloat16)
    return np.stack([head, tail])


def tables(size):
    index = np.arange(size)
    dft = np.exp(-2j * math.pi / size * (index[:, None] * index[None, :] % size)) / math.sqrt(size)
    freq = (index + size // 2) % size - size // 2
    phase = np.exp(-1j * FRESNEL * math.pi / size * freq.astype(np.float64) ** 2)
    prop = dft.conj() @ (phase[:, None] * dft)
    prop = 0.5 * (prop + prop.T)
    out = []
    for m in (prop, dft):
        right = np.block([[m.real, m.imag], [-m.imag, m.real]])
        out += [split_table(right), split_table(right.T)]
    return out


def halves(x):
    head = x.astype(jnp.bfloat16)
    tail = (x - head.astype(jnp.float32)).astype(jnp.bfloat16)
    return head, tail


def dot(a, b):
    return jnp.dot(a, b, preferred_element_type=jnp.float32)


def two_sided(re, im, right, left, slots, size):
    head, tail = halves(jnp.concatenate([re, im], axis=1))
    y = dot(head, right[0]) + dot(tail, right[0]) + dot(head, right[1])
    z = jnp.concatenate(
        [
            jnp.concatenate(
                [y[j * size : (j + 1) * size, :size], y[j * size : (j + 1) * size, size:]], axis=0
            )
            for j in range(slots)
        ],
        axis=1,
    )
    head, tail = halves(z)
    y = dot(left[0], head) + dot(left[0], tail) + dot(left[1], head)
    out_re = [y[:size, j * size : (j + 1) * size] for j in range(slots)]
    out_im = [y[size:, j * size : (j + 1) * size] for j in range(slots)]
    return jnp.concatenate(out_re, axis=0), jnp.concatenate(out_im, axis=0)


def axis_places():
    depth = lax.axis_index("depth")
    tile = lax.axis_index("tile")
    return depth, tile, lax.rem(tile, 2)


def gather_kernel(own_cols, near_place, far_place, trans, *outs):
    depth, _, _ = axis_places()
    blocks = trans.shape[2] // LANES
    shape = (trans.shape[0], trans.shape[1], LANES)
    lane = lax.broadcasted_iota(jnp.int32, shape, 2)
    for which in range(3):
        for rel in range(2):
            out = outs[2 * which + rel]

            def one(j, carry, which=which, rel=rel, out=out):
                slot = 2 * j + (depth if rel == 0 else 1 - depth)
                col = own_cols[slot] if which == 0 else (near_place, far_place)[which - 1][1, slot]
                block = col // LANES
                after = jnp.minimum(block + 1, blocks - 1)
                x = trans[:, :, pl.ds(pl.multiple_of(block * LANES, LANES), LANES)]
                y = trans[:, :, pl.ds(pl.multiple_of(after * LANES, LANES), LANES)]
                out[j] = jnp.where(lane >= col - block * LANES, x, y)
                return carry

            lax.fori_loop(0, out.shape[0], one, 0)


MESH = pl.DeviceIdType.MESH


def main_kernel(
    own_rows, own_cols, counts, near_place, probe, diff,
    own_k, own_g, near_k, near_g, far_k, far_g, a_right, a_left, f_right, f_left,
    own_k_out, own_g_out, near_k_out, near_g_out, far_k_out, far_g_out, probe_out,
    hopped, merged, rim_in, give_in, rim_back, own_in, rim_grad, own_grad, patch, psi,
    probe_part, probe_got, send_sem, recv_sem,
):
    depth, tile, odd = axis_places()
    tiles = lax.axis_size("tile")
    filled = counts[tile]
    rounds, arrays, half, size = own_k.shape
    group = arrays // 2
    slices = 2 * group
    pair = patch.shape[2] // size

    def flipped(bit):
        return tile + bit - 2 * bit * lax.rem(lax.div(tile, bit), 2)

    other = (1 - depth, tile)
    beside = (depth, flipped(1))
    onward = (depth, lax.rem(tile + 4 * odd - 2 + tiles, tiles))
    backward = (depth, lax.rem(tile - 4 * odd + 2 + tiles, tiles))
    bits = []
    while 2 ** len(bits) < tiles:
        bits.append(2 ** len(bits))
    bits = bits[::-1]

    barrier = pltpu.get_barrier_semaphore()
    greeted = [other, beside, onward, backward] + [(depth, flipped(b)) for b in bits if b > 2]
    for device in greeted:
        pl.semaphore_signal(barrier, inc=1, device_id=device, device_id_type=MESH)
    pl.semaphore_wait(barrier, len(greeted))

    def copy(src, dst, device, sem):
        return pltpu.make_async_remote_copy(
            src_ref=src, dst_ref=dst, send_sem=send_sem.at[sem], recv_sem=recv_sem.at[sem],
            device_id=device, device_id_type=MESH,
        )

    def hop_in(rel, j):
        return copy((far_k, far_g)[rel].at[j], hopped.at[rel, j], onward, rel * rounds + j)

    def cross_in(rel, j):
        dst = give_in.at[j] if rel else rim_in.at[0, j]
        return copy(merged.at[rel, j], dst, beside, (2 + rel) * rounds + j)

    def own_swap(j):
        return copy(own_g.at[j], own_in.at[1, j], other, 4 * rounds + j)

    def rim_swap(j):
        return copy(give_in.at[j], rim_in.at[1, j], other, 5 * rounds + j)

    def own_return(j):
        return copy(own_grad.at[1, j], own_g_out.at[j], other, 6 * rounds + j)

    def rim_return(j):
        return copy(rim_grad.at[1, j], rim_back.at[j], other, 7 * rounds + j)

    def cross_out(rel, j):
        src = rim_back.at[j] if rel else rim_grad.at[0, j]
        return copy(src, (near_k_out, near_g_out)[rel].at[j], beside, (8 + rel) * rounds + j)

    def hop_out(rel, j):
        refs = ((near_k_out, far_k_out), (near_g_out, far_g_out))[rel]
        return copy(refs[0].at[j], refs[1].at[j], backward, (10 + rel) * rounds + j)

    def probe_swap():
        return copy(probe_part.at[1 - depth], probe_got.at[0], other, 12 * rounds)

    def probe_step(i):
        device = (depth, flipped(bits[i]))
        return copy(probe_part.at[2 + i], probe_got.at[1 + i], device, 12 * rounds + 1 + i)

    for j in range(rounds):
        hop_in(1, j).start()
        hop_in(0, j).start()
    for j in range(rounds):
        own_swap(j).start()
    own_in[0] = own_k[...]
    row = lax.broadcasted_iota(jnp.int32, (arrays, half, size), 1)
    near_tile = tile + 1 - 2 * odd

    def merge(j, carry):
        for rel in (1, 0):
            hop_in(rel, j).wait_recv()
            slot = 2 * j + (1 - depth if rel else depth)
            begin = near_place[0, slot] - (near_tile - 1) * half
            near, far = (near_k, near_g)[rel][j], hopped[rel, j]
            near_rows = (row >= begin).astype(jnp.int32) != odd
            merged[rel, j] = jnp.where(near_rows, near, far)
            cross_in(rel, j).start()
        return carry

    lax.fori_loop(0, rounds, merge, 0)

    def pass_on(j, carry):
        cross_in(1, j).wait_recv()
        rim_swap(j).start()
        return carry

    def times(a, b):
        return a[0] * b[0] - a[1] * b[1], a[0] * b[1] + a[1] * b[0]

    def load(ref, s):
        return ref[s, 0], ref[s, 1]

    def apply(wave, right, left):
        return two_sided(wave[0], wave[1], right, left, pair, size)

    def rows(i):
        return slice(i * size, (i + 1) * size)

    def waves(p, carry):
        lax.fori_loop(p * pair, p * pair + pair, pass_on, 0)
        spots = []
        for i in range(pair):
            j = p * pair + i
            slot = 2 * j + depth
            down = own_rows[slot] - (tile - 1) * half
            across = lax.rem(own_cols[slot], LANES)
            spots.append((j, slot, down, across, slot < filled))
            for part in range(2):
                psi[0, part, rows(i), :] = pltpu.roll(pltpu.roll(probe[part], down, 0), across, 1)
        for i in range(pair):
            j = spots[i][0]
            cross_in(0, j).wait_recv()
            own_swap(j).wait_recv()
            rim_swap(j).wait_recv()
            for s in range(slices):
                side = lax.rem(depth + s // group, 2)
                for part in range(2):
                    a = part * group + s % group
                    patch[s, part, i * size : i * size + half, :] = rim_in[side, j, a]
                    patch[s, part, i * size + half : (i + 1) * size, :] = own_in[side, j, a]

        def forward(s, carry):
            wave = apply(times(load(patch, s), load(psi, s)), a_right, a_left)
            psi[s + 1, 0] = wave[0]
            psi[s + 1, 1] = wave[1]
            return carry

        lax.fori_loop(0, slices - 1, forward, 0)
        far = apply(times(load(patch, slices - 1), load(psi, slices - 1)), f_right, f_left)
        measured = jnp.concatenate([diff[spot[1]] for spot in spots], axis=0)
        misfit = far[0] * far[0] + far[1] * far[1] - measured

        def finish(s, along):
            term = times(load(psi, s), along)
            term = (term[0], -term[1])
            side = lax.rem(depth + lax.div(s, group), 2)
            for i, (j, _, _, _, on) in enumerate(spots):
                for part in range(2):
                    a = part * group + lax.rem(s, group)
                    value = jnp.where(on, term[part][rows(i)], 0.0)
                    rim_grad[side, j, a] = value[:half]
                    own_grad[side, j, a] = value[half:]
            return times(load(patch, s), along)

        back = apply((misfit * far[0], -(misfit * far[1])), f_right, f_left)
        back = finish(jnp.int32(slices - 1), back)

        def reverse(n, back):
            return finish(slices - 2 - n, apply(back, a_right, a_left))

        back = lax.fori_loop(0, slices - 1, reverse, back)
        for i in range(pair):
            j = spots[i][0]
            rim_return(j).start()
            cross_out(0, j).start()
            own_return(j).start()
        for part in range(2):
            total = jnp.zeros((size, size), jnp.float32)
            for i, (_, _, down, across, on) in enumerate(spots):
                value = jnp.where(on, back[part][rows(i)], 0.0)
                value = pltpu.roll(value, lax.rem(size - down, size), 0)
                total = total + pltpu.roll(value, lax.rem(size - across, size), 1)
            total = total if part == 0 else -total
            for side in range(2):
                before = probe_part[side, part]
                probe_part[side, part] = before + total[side * half : (side + 1) * half]
        return carry

    probe_part[0] = jnp.zeros_like(probe_part[0])
    probe_part[1] = jnp.zeros_like(probe_part[1])
    lax.fori_loop(0, rounds // pair, waves, 0)

    probe_swap().start()

    def give(j, carry):
        rim_return(j).wait_recv()
        cross_out(1, j).start()
        return carry

    lax.fori_loop(0, rounds, give, 0)
    probe_swap().wait_recv()
    probe_part[2] = probe_part[depth] + probe_got[0]
    probe_step(0).start()

    done = 0
    for rel, first in ((0, 0), (0, rounds // 2), (1, 0), (1, rounds // 2)):

        def onto(j, carry, rel=rel):
            cross_out(rel, j).wait_recv()
            hop_out(rel, j).start()
            return carry

        lax.fori_loop(first, first + rounds // 2, onto, 0)
        if done < len(bits) - 1:
            probe_step(done).wait_recv()
            probe_part[3 + done] = probe_part[2 + done] + probe_got[1 + done]
            done += 1
            probe_step(done).start()
    while done < len(bits):
        probe_step(done).wait_recv()
        probe_part[3 + done] = probe_part[2 + done] + probe_got[1 + done]
        done += 1
        if done < len(bits):
            probe_step(done).start()
    probe_out[...] = probe_part[2 + len(bits)]
    own_k_out[...] = own_grad[0]

    def drain(j, carry):
        own_return(j).wait_recv()
        for rel in range(2):
            hop_out(rel, j).wait_recv()
            hop_in(rel, j).wait_send()
            cross_out(rel, j).wait_send()
            hop_out(rel, j).wait_send()
            cross_in(rel, j).wait_send()
        own_swap(j).wait_send()
        rim_swap(j).wait_send()
        own_return(j).wait_send()
        rim_return(j).wait_send()
        return carry

    lax.fori_loop(0, rounds, drain, 0)
    probe_swap().wait_send()
    for i in range(len(bits)):
        probe_step(i).wait_send()


def scatter_kernel(own_cols, near_place, far_place, own_k, own_g, near_k, near_g, far_k, far_g, out):
    depth, tile, odd = axis_places()
    blocks = out.shape[2] // LANES
    shape = (out.shape[0], out.shape[1], LANES)
    lane = lax.broadcasted_iota(jnp.int32, shape, 2)
    row = lax.broadcasted_iota(jnp.int32, shape, 1)
    out[...] = jnp.zeros_like(out)
    for index, ref in enumerate((own_k, own_g, near_k, near_g, far_k, far_g)):
        which, rel = index // 2, index % 2

        def one(j, carry, which=which, rel=rel, ref=ref):
            slot = 2 * j + (depth if rel == 0 else 1 - depth)
            value = ref[j]
            col = own_cols[slot] if which == 0 else (near_place, far_place)[which - 1][1, slot]
            if which:
                under = odd if which == 1 else 1 - odd
                place = (near_place, far_place)[which - 1]
                owner = tile + (1 - 2 * odd if which == 1 else 2 * odd - 1)
                start = place[0, slot] - (owner - 1) * shape[1]
                low = jnp.where(under == 1, 0, start)
                high = jnp.where(under == 1, start, shape[1])
                exists = (owner >= 0) & (owner < lax.axis_size("tile"))
                high = jnp.where(exists, high, low)
                value = jnp.where((row >= low) & (row < high), value, 0.0)
            block = col // LANES
            after = jnp.minimum(block + 1, blocks - 1)
            inside = lane >= col - block * LANES
            at = pl.ds(pl.multiple_of(block * LANES, LANES), LANES)
            out[:, :, at] = out[:, :, at] + jnp.where(inside, value, 0.0)
            at = pl.ds(pl.multiple_of(after * LANES, LANES), LANES)
            out[:, :, at] = out[:, :, at] + jnp.where(inside, 0.0, value)
            return carry

        lax.fori_loop(0, ref.shape[0], one, 0)


SMEM = pl.BlockSpec(memory_space=pltpu.SMEM)
VMEM = pl.BlockSpec(memory_space=pltpu.VMEM)
PARAMS = pltpu.CompilerParams(vmem_limit_bytes=48 * 1024 * 1024)


def shards(transmission, probe, scan_rows, scan_cols, tile_counts, diffraction):
    size = probe.shape[-1]
    half = size // 2
    group, strip, cols = transmission.shape[1:]
    rounds = scan_rows.shape[0] // 2
    tiles = lax.axis_size("tile")
    f32 = jnp.float32

    beside = [(c, c ^ 1) for c in range(tiles)]
    across = [(c, c + 1 if c % 2 else c - 1) for c in range(1, tiles - 1)]

    place = jnp.stack([scan_rows, scan_cols])
    place_near = lax.ppermute(place, "tile", beside)
    place_far = lax.ppermute(place, "tile", across)

    flat = transmission.reshape(2 * group, strip, cols)
    piece = jax.ShapeDtypeStruct((rounds, 2 * group, strip, LANES), f32)
    own_k, own_g, near_k, near_g, far_k, far_g = pl.pallas_call(
        gather_kernel,
        out_shape=[piece] * 6,
        in_specs=[SMEM] * 3 + [VMEM],
        out_specs=[VMEM] * 6,
        compiler_params=PARAMS,
        name="gather",
    )(scan_cols, place_near, place_far, flat)

    tabs = [jnp.asarray(t) for t in tables(size)]
    pair = 2
    stages = (tiles - 1).bit_length()
    sems = pltpu.SemaphoreType.DMA((12 * rounds + 1 + stages,))
    both = pltpu.VMEM((2,) + piece.shape, f32)
    single = pltpu.VMEM(piece.shape, f32)
    waves = pltpu.VMEM((2 * group, 2, pair * size, size), f32)
    rows_shape = (probe.shape[0], half, size)
    *parts, probe_grad = pl.pallas_call(
        main_kernel,
        out_shape=[piece] * 6 + [jax.ShapeDtypeStruct(rows_shape, f32)],
        in_specs=[SMEM] * 4 + [VMEM] * 12,
        out_specs=[VMEM] * 7,
        scratch_shapes=[both, both, both, single, single, both, both, both]
        + [waves, waves]
        + [pltpu.VMEM((3 + stages,) + rows_shape, f32), pltpu.VMEM((1 + stages,) + rows_shape, f32)]
        + [sems, sems],
        compiler_params=pltpu.CompilerParams(
            vmem_limit_bytes=48 * 1024 * 1024, collective_id=0, has_side_effects=True
        ),
        name="waves",
    )(
        scan_rows, scan_cols, tile_counts, place_near, probe, diffraction,
        own_k, own_g, near_k, near_g, far_k, far_g, *tabs,
    )

    grads = pl.pallas_call(
        scatter_kernel,
        out_shape=jax.ShapeDtypeStruct(flat.shape, f32),
        in_specs=[SMEM] * 3 + [VMEM] * 6,
        out_specs=VMEM,
        compiler_params=PARAMS,
        name="scatter",
    )(scan_cols, place_near, place_far, *parts)
    return (grads.reshape(transmission.shape), probe_grad)


def solution(mesh):
    placed = (P(None, "depth", "tile", None), P(), P("tile"), P("tile"), P(), P("tile", None, None))
    return jax.shard_map(
        shards,
        mesh=mesh,
        in_specs=placed,
        out_specs=(P(None, "depth", "tile", None), P(None, "depth", None)),
        check_vma=False,
    )
```

```python
import math

import jax
import jax.numpy as jnp
import ml_dtypes
import numpy as np
from jax import lax
from jax.experimental import pallas as pl
from jax.experimental.pallas import tpu as pltpu
from jax.sharding import PartitionSpec as P

FRESNEL = 0.5
LANES = 128


def split_table(table):
    head = table.astype(np.float32).astype(ml_dtypes.bfloat16)
    tail = (table - head.astype(np.float64)).astype(np.float32).astype(ml_dtypes.bfloat16)
    return np.stack([head, tail])


def tables(size):
    index = np.arange(size)
    dft = np.exp(-2j * math.pi / size * (index[:, None] * index[None, :] % size)) / math.sqrt(size)
    freq = (index + size // 2) % size - size // 2
    phase = np.exp(-1j * FRESNEL * math.pi / size * freq.astype(np.float64) ** 2)
    prop = dft.conj() @ (phase[:, None] * dft)
    prop = 0.5 * (prop + prop.T)
    out = []
    for m in (prop, dft):
        right = np.block([[m.real, m.imag], [-m.imag, m.real]])
        out += [split_table(right), split_table(right.T)]
    return out


def halves(x):
    head = x.astype(jnp.bfloat16)
    tail = (x - head.astype(jnp.float32)).astype(jnp.bfloat16)
    return head, tail


def dot(a, b):
    return jnp.dot(a, b, preferred_element_type=jnp.float32)


def two_sided(re, im, right, left, slots, size):
    head, tail = halves(jnp.concatenate([re, im], axis=1))
    y = dot(head, right[0]) + dot(tail, right[0]) + dot(head, right[1])
    z = jnp.concatenate(
        [
            jnp.concatenate(
                [y[j * size : (j + 1) * size, :size], y[j * size : (j + 1) * size, size:]], axis=0
            )
            for j in range(slots)
        ],
        axis=1,
    )
    head, tail = halves(z)
    y = dot(left[0], head) + dot(left[0], tail) + dot(left[1], head)
    out_re = [y[:size, j * size : (j + 1) * size] for j in range(slots)]
    out_im = [y[size:, j * size : (j + 1) * size] for j in range(slots)]
    return jnp.concatenate(out_re, axis=0), jnp.concatenate(out_im, axis=0)


def axis_places():
    depth = lax.axis_index("depth")
    tile = lax.axis_index("tile")
    return depth, tile, lax.rem(tile, 2)


def gather_kernel(own_cols, near_place, far_place, trans, *outs):
    depth, _, _ = axis_places()
    blocks = trans.shape[2] // LANES
    shape = (trans.shape[0], trans.shape[1], LANES)
    lane = lax.broadcasted_iota(jnp.int32, shape, 2)
    for which in range(3):
        for rel in range(2):
            out = outs[2 * which + rel]

            def one(j, carry, which=which, rel=rel, out=out):
                slot = 2 * j + (depth if rel == 0 else 1 - depth)
                col = own_cols[slot] if which == 0 else (near_place, far_place)[which - 1][1, slot]
                block = col // LANES
                after = jnp.minimum(block + 1, blocks - 1)
                x = trans[:, :, pl.ds(pl.multiple_of(block * LANES, LANES), LANES)]
                y = trans[:, :, pl.ds(pl.multiple_of(after * LANES, LANES), LANES)]
                out[j] = jnp.where(lane >= col - block * LANES, x, y)
                return carry

            lax.fori_loop(0, out.shape[0], one, 0)


MESH = pl.DeviceIdType.MESH


def main_kernel(
    own_rows, own_cols, counts, near_place, probe, diff,
    own_k, own_g, near_k, near_g, far_k, far_g, a_right, a_left, f_right, f_left,
    own_k_out, own_g_out, near_k_out, near_g_out, far_k_out, far_g_out, probe_out,
    hopped, merged, rim_in, give_in, rim_back, own_in, near_in, rim_grad, own_grad, patch, psi, hold,
    probe_part, probe_got, send_sem, recv_sem, load_sem,
):
    depth, tile, odd = axis_places()
    tiles = lax.axis_size("tile")
    filled = counts[tile]
    rounds, arrays, half, size = own_k.shape
    group = arrays // 2
    slices = 2 * group
    pair = patch.shape[2] // size

    def flipped(bit):
        return tile + bit - 2 * bit * lax.rem(lax.div(tile, bit), 2)

    other = (1 - depth, tile)
    beside = (depth, flipped(1))
    onward = (depth, lax.rem(tile + 4 * odd - 2 + tiles, tiles))
    backward = (depth, lax.rem(tile - 4 * odd + 2 + tiles, tiles))
    bits = []
    while 2 ** len(bits) < tiles:
        bits.append(2 ** len(bits))
    bits = bits[::-1]

    loads = [
        pltpu.make_async_copy(src, dst, load_sem.at[i])
        for i, (src, dst) in enumerate(
            ((near_g, near_in.at[1]), (near_k, near_in.at[0]), (own_k, own_in.at[0]))
        )
    ]
    for local in loads:
        local.start()
    barrier = pltpu.get_barrier_semaphore()
    greeted = [other, beside, onward, backward] + [(depth, flipped(b)) for b in bits if b > 2]
    for device in greeted:
        pl.semaphore_signal(barrier, inc=1, device_id=device, device_id_type=MESH)
    pl.semaphore_wait(barrier, len(greeted))

    def copy(src, dst, device, sem):
        return pltpu.make_async_remote_copy(
            src_ref=src, dst_ref=dst, send_sem=send_sem.at[sem], recv_sem=recv_sem.at[sem],
            device_id=device, device_id_type=MESH,
        )

    def hop_in(rel, j):
        return copy((far_k, far_g)[rel].at[j], hopped.at[rel, j], onward, rel * rounds + j)

    def cross_in(rel, j):
        dst = give_in.at[j] if rel else rim_in.at[0, j]
        return copy(merged.at[rel, j], dst, beside, (2 + rel) * rounds + j)

    def own_swap(j):
        return copy(own_g.at[j], own_in.at[1, j], other, 4 * rounds + j)

    def rim_swap(j):
        return copy(give_in.at[j], rim_in.at[1, j], other, 5 * rounds + j)

    def own_return(j):
        return copy(own_grad.at[1, j], own_g_out.at[j], other, 6 * rounds + j)

    def rim_return(j):
        return copy(rim_grad.at[1, j], rim_back.at[j], other, 7 * rounds + j)

    def cross_out(rel, j):
        src = rim_back.at[j] if rel else rim_grad.at[0, j]
        return copy(src, (near_k_out, near_g_out)[rel].at[j], beside, (8 + rel) * rounds + j)

    def hop_out(rel, j):
        refs = ((near_k_out, far_k_out), (near_g_out, far_g_out))[rel]
        return copy(refs[0].at[j], refs[1].at[j], backward, (10 + rel) * rounds + j)

    def probe_swap():
        return copy(probe_part.at[1 - depth], probe_got.at[0], other, 12 * rounds)

    def probe_step(i):
        device = (depth, flipped(bits[i]))
        return copy(probe_part.at[2 + i], probe_got.at[1 + i], device, 12 * rounds + 1 + i)

    order = [(rel, j) for j in range(rounds) for rel in (1, 0)]
    for item in order[:2]:
        hop_in(*item).start()
    for j in range(rounds):
        own_swap(j).start()
    for local in loads:
        local.wait()
    row = lax.broadcasted_iota(jnp.int32, (arrays, half, size), 1)
    near_tile = tile + 1 - 2 * odd

    def merge(i):
        rel, j = order[i]
        hop_in(rel, j).wait_send()
        if i + 2 < len(order):
            hop_in(*order[i + 2]).start()
        hop_in(rel, j).wait_recv()
        slot = 2 * j + (1 - depth if rel else depth)
        begin = near_place[0, slot] - (near_tile - 1) * half
        near_rows = (row >= begin).astype(jnp.int32) != odd
        merged[rel, j] = jnp.where(near_rows, near_in[rel, j], hopped[rel, j])
        cross_in(rel, j).start()

    def pass_on(j):
        cross_in(1, j).wait_recv()
        rim_swap(j).start()

    def times(a, b):
        return a[0] * b[0] - a[1] * b[1], a[0] * b[1] + a[1] * b[0]

    def load(ref, s):
        return ref[s, 0], ref[s, 1]

    def apply(wave, right, left):
        return two_sided(wave[0], wave[1], right, left, pair, size)

    def rows(i):
        return slice(i * size, (i + 1) * size)

    def waves(p):
        spots = []
        for i in range(pair):
            j = p * pair + i
            slot = 2 * j + depth
            down = own_rows[slot] - (tile - 1) * half
            across = lax.rem(own_cols[slot], LANES)
            spots.append((j, slot, down, across, slot < filled))
            for part in range(2):
                psi[0, part, rows(i), :] = pltpu.roll(pltpu.roll(probe[part], down, 0), across, 1)
        for i in range(pair):
            j = spots[i][0]
            cross_in(0, j).wait_recv()
            own_swap(j).wait_recv()
            rim_swap(j).wait_recv()
            for s in range(slices):
                side = lax.rem(depth + s // group, 2)
                for part in range(2):
                    a = part * group + s % group
                    patch[s, part, i * size : i * size + half, :] = rim_in[side, j, a]
                    patch[s, part, i * size + half : (i + 1) * size, :] = own_in[side, j, a]
        for s in range(slices - 1):
            wave = apply(times(load(patch, s), load(psi, s)), a_right, a_left)
            psi[s + 1, 0] = wave[0]
            psi[s + 1, 1] = wave[1]
            if s == 0:
                yield
        s = slices - 1
        far = apply(times(load(patch, s), load(psi, s)), f_right, f_left)
        measured = jnp.concatenate([diff[spot[1]] for spot in spots], axis=0)
        misfit = far[0] * far[0] + far[1] * far[1] - measured
        hold[0] = misfit * far[0]
        hold[1] = -(misfit * far[1])
        yield
        for s in reversed(range(slices)):
            tabs = (f_right, f_left) if s == slices - 1 else (a_right, a_left)
            along = apply((hold[0], hold[1]), *tabs)
            term = times(load(psi, s), along)
            term = (term[0], -term[1])
            side = lax.rem(depth + s // group, 2)
            for i, (j, _, _, _, on) in enumerate(spots):
                for part in range(2):
                    a = part * group + s % group
                    value = jnp.where(on, term[part][rows(i)], 0.0)
                    rim_grad[side, j, a] = value[:half]
                    own_grad[side, j, a] = value[half:]
            back = times(load(patch, s), along)
            hold[0] = back[0]
            hold[1] = back[1]
            if s == 2:
                yield
        for i in range(pair):
            j = spots[i][0]
            rim_return(j).start()
            own_return(j).start()
        yield
        for part in range(2):
            total = jnp.zeros((size, size), jnp.float32)
            for i, (_, _, down, across, on) in enumerate(spots):
                value = jnp.where(on, hold[part, rows(i), :], 0.0)
                value = pltpu.roll(value, lax.rem(size - down, size), 0)
                total = total + pltpu.roll(value, lax.rem(size - across, size), 1)
            total = total if part == 0 else -total
            for side in range(2):
                value = total[side * half : (side + 1) * half]
                if p:
                    value = value + probe_part[side, part]
                probe_part[side, part] = value

    first = waves(0)
    for i in range(len(order)):
        merge(i)
        if i == 4:
            pass_on(0)
            pass_on(1)
        if i >= 5:
            next(first)
    pass_on(2)
    pass_on(3)
    next(first)

    back_order = [(0, 0), (0, 1), (1, 0), (1, 1), (0, 2), (0, 3), (1, 2), (1, 3)]

    def send_back(i):
        if i < len(back_order):
            rel, j = back_order[i]
            if rel:
                rim_return(j).wait_recv()
            cross_out(rel, j).start()

    def onto(i):
        cross_out(*back_order[i]).wait_send()
        send_back(i + 2)
        cross_out(*back_order[i]).wait_recv()
        hop_out(*back_order[i]).start()

    send_back(0)
    send_back(1)
    next(first, None)
    second = waves(1)
    next(second)
    next(second)
    next(second)
    onto(0)
    onto(1)
    next(second)
    onto(2)
    next(second, None)

    probe_swap().start()

    probe_swap().wait_recv()
    probe_part[2] = probe_part[depth] + probe_got[0]
    probe_step(0).start()

    done = 0
    for i in range(3, len(back_order)):
        onto(i)
        if done < len(bits) - 1:
            probe_step(done).wait_recv()
            probe_part[3 + done] = probe_part[2 + done] + probe_got[1 + done]
            done += 1
            probe_step(done).start()
    while done < len(bits):
        probe_step(done).wait_recv()
        probe_part[3 + done] = probe_part[2 + done] + probe_got[1 + done]
        done += 1
        if done < len(bits):
            probe_step(done).start()
    probe_out[...] = probe_part[2 + len(bits)]
    own_k_out[...] = own_grad[0]

    def drain(j, carry):
        own_return(j).wait_recv()
        for rel in range(2):
            hop_out(rel, j).wait_recv()
            hop_out(rel, j).wait_send()
            cross_in(rel, j).wait_send()
        own_swap(j).wait_send()
        rim_swap(j).wait_send()
        own_return(j).wait_send()
        rim_return(j).wait_send()
        return carry

    lax.fori_loop(0, rounds, drain, 0)
    probe_swap().wait_send()
    for i in range(len(bits)):
        probe_step(i).wait_send()


def scatter_kernel(own_cols, near_place, far_place, own_k, own_g, near_k, near_g, far_k, far_g, out):
    depth, tile, odd = axis_places()
    blocks = out.shape[2] // LANES
    shape = (out.shape[0], out.shape[1], LANES)
    lane = lax.broadcasted_iota(jnp.int32, shape, 2)
    row = lax.broadcasted_iota(jnp.int32, shape, 1)
    out[...] = jnp.zeros_like(out)
    for index, ref in enumerate((own_k, own_g, near_k, near_g, far_k, far_g)):
        which, rel = index // 2, index % 2

        def one(j, carry, which=which, rel=rel, ref=ref):
            slot = 2 * j + (depth if rel == 0 else 1 - depth)
            value = ref[j]
            col = own_cols[slot] if which == 0 else (near_place, far_place)[which - 1][1, slot]
            if which:
                under = odd if which == 1 else 1 - odd
                place = (near_place, far_place)[which - 1]
                owner = tile + (1 - 2 * odd if which == 1 else 2 * odd - 1)
                start = place[0, slot] - (owner - 1) * shape[1]
                low = jnp.where(under == 1, 0, start)
                high = jnp.where(under == 1, start, shape[1])
                exists = (owner >= 0) & (owner < lax.axis_size("tile"))
                high = jnp.where(exists, high, low)
                value = jnp.where((row >= low) & (row < high), value, 0.0)
            block = col // LANES
            after = jnp.minimum(block + 1, blocks - 1)
            inside = lane >= col - block * LANES
            at = pl.ds(pl.multiple_of(block * LANES, LANES), LANES)
            out[:, :, at] = out[:, :, at] + jnp.where(inside, value, 0.0)
            at = pl.ds(pl.multiple_of(after * LANES, LANES), LANES)
            out[:, :, at] = out[:, :, at] + jnp.where(inside, 0.0, value)
            return carry

        lax.fori_loop(0, ref.shape[0], one, 0)


SMEM = pl.BlockSpec(memory_space=pltpu.SMEM)
VMEM = pl.BlockSpec(memory_space=pltpu.VMEM)
ANY = pl.BlockSpec(memory_space=pl.ANY)
PARAMS = pltpu.CompilerParams(vmem_limit_bytes=48 * 1024 * 1024)


def shards(transmission, probe, scan_rows, scan_cols, tile_counts, diffraction):
    size = probe.shape[-1]
    half = size // 2
    group, strip, cols = transmission.shape[1:]
    rounds = scan_rows.shape[0] // 2
    tiles = lax.axis_size("tile")
    f32 = jnp.float32

    beside = [(c, c ^ 1) for c in range(tiles)]
    across = [(c, c + 1 if c % 2 else c - 1) for c in range(1, tiles - 1)]

    place = jnp.stack([scan_rows, scan_cols])
    place_near = lax.ppermute(place, "tile", beside)
    place_far = lax.ppermute(place, "tile", across)

    flat = transmission.reshape(2 * group, strip, cols)
    piece = jax.ShapeDtypeStruct((rounds, 2 * group, strip, LANES), f32)
    own_k, own_g, near_k, near_g, far_k, far_g = pl.pallas_call(
        gather_kernel,
        out_shape=[piece] * 6,
        in_specs=[SMEM] * 3 + [VMEM],
        out_specs=[VMEM] * 6,
        compiler_params=PARAMS,
        name="gather",
    )(scan_cols, place_near, place_far, flat)

    tabs = [jnp.asarray(t) for t in tables(size)]
    pair = 2
    stages = (tiles - 1).bit_length()
    sems = pltpu.SemaphoreType.DMA((12 * rounds + 1 + stages,))
    both = pltpu.VMEM((2,) + piece.shape, f32)
    single = pltpu.VMEM(piece.shape, f32)
    waves = pltpu.VMEM((2 * group, 2, pair * size, size), f32)
    rows_shape = (probe.shape[0], half, size)
    *parts, probe_grad = pl.pallas_call(
        main_kernel,
        out_shape=[piece] * 6 + [jax.ShapeDtypeStruct(rows_shape, f32)],
        in_specs=[SMEM] * 4 + [VMEM] * 2 + [ANY] * 6 + [VMEM] * 4,
        out_specs=[VMEM] * 7,
        scratch_shapes=[both, both, both, single, single, both, both, both, both]
        + [waves, waves, pltpu.VMEM((2, pair * size, size), f32)]
        + [pltpu.VMEM((3 + stages,) + rows_shape, f32), pltpu.VMEM((1 + stages,) + rows_shape, f32)]
        + [sems, sems, pltpu.SemaphoreType.DMA((3,))],
        compiler_params=pltpu.CompilerParams(
            vmem_limit_bytes=48 * 1024 * 1024, collective_id=0, has_side_effects=True
        ),
        name="waves",
    )(
        scan_rows, scan_cols, tile_counts, place_near, probe, diffraction,
        own_k, own_g, near_k, near_g, far_k, far_g, *tabs,
    )

    grads = pl.pallas_call(
        scatter_kernel,
        out_shape=jax.ShapeDtypeStruct(flat.shape, f32),
        in_specs=[SMEM] * 3 + [VMEM] * 6,
        out_specs=VMEM,
        compiler_params=PARAMS,
        name="scatter",
    )(scan_cols, place_near, place_far, *parts)
    return (grads.reshape(transmission.shape), probe_grad)


def solution(mesh):
    placed = (P(None, "depth", "tile", None), P(), P("tile"), P("tile"), P(), P("tile", None, None))
    return jax.shard_map(
        shards,
        mesh=mesh,
        in_specs=placed,
        out_specs=(P(None, "depth", "tile", None), P(None, "depth", None)),
        check_vma=False,
    )
```

```python
import math

import jax
import jax.numpy as jnp
import ml_dtypes
import numpy as np
from jax import lax
from jax.experimental import pallas as pl
from jax.experimental.pallas import tpu as pltpu
from jax.sharding import PartitionSpec as P

FRESNEL = 0.5
LANES = 128


def split_table(table):
    head = table.astype(np.float32).astype(ml_dtypes.bfloat16)
    tail = (table - head.astype(np.float64)).astype(np.float32).astype(ml_dtypes.bfloat16)
    return np.concatenate([head, tail])


def tables(size):
    index = np.arange(size)
    dft = np.exp(-2j * math.pi / size * (index[:, None] * index[None, :] % size)) / math.sqrt(size)
    freq = (index + size // 2) % size - size // 2
    phase = np.exp(-1j * FRESNEL * math.pi / size * freq.astype(np.float64) ** 2)
    prop = dft.conj() @ (phase[:, None] * dft)
    prop = 0.5 * (prop + prop.T)
    out = []
    for m in (prop, dft):
        right = np.block([[m.real, m.imag], [-m.imag, m.real]])
        out += [split_table(right), split_table(right.T)]
    return out


def halves(x):
    head = x.astype(jnp.bfloat16)
    tail = (x - head.astype(jnp.float32)).astype(jnp.bfloat16)
    return head, tail


def dot(a, b):
    return jnp.dot(a, b, preferred_element_type=jnp.float32)


def two_sided(re, im, right, left, slots, size):
    count = slots * size
    head, tail = halves(jnp.concatenate([re, im], axis=1))
    y = dot(jnp.concatenate([head, tail], axis=0), right[: 2 * size])
    y = y[:count] + y[count:] + dot(head, right[2 * size :])
    z = jnp.concatenate(
        [
            jnp.concatenate(
                [y[j * size : (j + 1) * size, :size], y[j * size : (j + 1) * size, size:]], axis=0
            )
            for j in range(slots)
        ],
        axis=1,
    )
    head, tail = halves(z)
    y = dot(left[...], head)
    y = y[: 2 * size] + y[2 * size :] + dot(left[: 2 * size], tail)
    out_re = [y[:size, j * size : (j + 1) * size] for j in range(slots)]
    out_im = [y[size:, j * size : (j + 1) * size] for j in range(slots)]
    return jnp.concatenate(out_re, axis=0), jnp.concatenate(out_im, axis=0)


def axis_places():
    depth = lax.axis_index("depth")
    tile = lax.axis_index("tile")
    return depth, tile, lax.rem(tile, 2)


def gather_kernel(own_cols, near_place, far_place, trans, *outs):
    depth, _, _ = axis_places()
    blocks = trans.shape[2] // LANES
    shape = (trans.shape[0], trans.shape[1], LANES)
    lane = lax.broadcasted_iota(jnp.int32, shape, 2)
    for which in range(3):
        for rel in range(2):
            out = outs[2 * which + rel]

            def one(j, carry, which=which, rel=rel, out=out):
                slot = 2 * j + (depth if rel == 0 else 1 - depth)
                col = own_cols[slot] if which == 0 else (near_place, far_place)[which - 1][1, slot]
                block = col // LANES
                after = jnp.minimum(block + 1, blocks - 1)
                x = trans[:, :, pl.ds(pl.multiple_of(block * LANES, LANES), LANES)]
                y = trans[:, :, pl.ds(pl.multiple_of(after * LANES, LANES), LANES)]
                out[j] = jnp.where(lane >= col - block * LANES, x, y)
                return carry

            lax.fori_loop(0, out.shape[0], one, 0)


MESH = pl.DeviceIdType.MESH


def main_kernel(
    own_rows, own_cols, counts, near_place, probe_hbm, diff_hbm,
    own_k, own_g, near_k, near_g, far_k, far_g, *rest,
):
    tables_hbm, rest = rest[:4], rest[4:]
    exchange(
        own_rows, own_cols, counts, near_place, probe_hbm, diff_hbm,
        own_k, own_g, near_k, near_g, far_k, far_g, tables_hbm, *rest,
    )


def exchange(
    own_rows, own_cols, counts, near_place, probe_hbm, diff_hbm,
    own_k, own_g, near_k, near_g, far_k, far_g, tables_hbm,
    own_k_out, own_g_out, near_k_out, near_g_out, far_k_out, far_g_out, probe_out,
    hopped, merged, rim_in, give_in, rim_back, own_in, near_in, rim_grad, own_grad, patch, psi, hold,
    probe_part, probe_got, probe, diff, a_right, a_left, f_right, f_left,
    send_sem, recv_sem, load_sem,
):
    depth, tile, odd = axis_places()
    tiles = lax.axis_size("tile")
    filled = counts[tile]
    rounds, arrays, half, size = own_k.shape
    group = arrays // 2
    slices = 2 * group
    pair = patch.shape[2] // size

    def flipped(bit):
        return tile + bit - 2 * bit * lax.rem(lax.div(tile, bit), 2)

    other = (1 - depth, tile)
    beside = (depth, flipped(1))
    onward = (depth, lax.rem(tile + 4 * odd - 2 + tiles, tiles))
    backward = (depth, lax.rem(tile - 4 * odd + 2 + tiles, tiles))
    bits = []
    while 2 ** len(bits) < tiles:
        bits.append(2 ** len(bits))
    bits = bits[::-1]

    loads = [
        pltpu.make_async_copy(src, dst, load_sem.at[i])
        for i, (src, dst) in enumerate(
            (
                (near_g, near_in.at[1]),
                (near_k, near_in.at[0]),
                (own_k, own_in.at[0]),
                (probe_hbm, probe),
                (diff_hbm, diff),
                *zip(tables_hbm, (a_right, a_left, f_right, f_left)),
            )
        )
    ]
    for local in loads:
        local.start()
    barrier = pltpu.get_barrier_semaphore()
    greeted = [other, beside, onward, backward] + [(depth, flipped(b)) for b in bits if b > 2]
    for device in greeted:
        pl.semaphore_signal(barrier, inc=1, device_id=device, device_id_type=MESH)
    pl.semaphore_wait(barrier, len(greeted))

    def copy(src, dst, device, sem):
        return pltpu.make_async_remote_copy(
            src_ref=src, dst_ref=dst, send_sem=send_sem.at[sem], recv_sem=recv_sem.at[sem],
            device_id=device, device_id_type=MESH,
        )

    def hop_in(rel, j):
        return copy((far_k, far_g)[rel].at[j], hopped.at[rel, j], onward, rel * rounds + j)

    def cross_in(rel, j):
        dst = give_in.at[j] if rel else rim_in.at[0, j]
        return copy(merged.at[rel, j], dst, beside, (2 + rel) * rounds + j)

    def own_swap(j):
        return copy(own_g.at[j], own_in.at[1, j], other, 4 * rounds + j)

    def rim_swap(j):
        return copy(give_in.at[j], rim_in.at[1, j], other, 5 * rounds + j)

    def own_return(j):
        return copy(own_grad.at[1, j], own_g_out.at[j], other, 6 * rounds + j)

    def rim_return(j):
        return copy(rim_grad.at[1, j], rim_back.at[j], other, 7 * rounds + j)

    def cross_out(rel, j):
        src = rim_back.at[j] if rel else rim_grad.at[0, j]
        return copy(src, (near_k_out, near_g_out)[rel].at[j], beside, (8 + rel) * rounds + j)

    def hop_out(rel, j):
        refs = ((near_k_out, far_k_out), (near_g_out, far_g_out))[rel]
        return copy(refs[0].at[j], refs[1].at[j], backward, (10 + rel) * rounds + j)

    def probe_swap():
        return copy(probe_part.at[1 - depth], probe_got.at[0], other, 12 * rounds)

    def probe_step(i):
        device = (depth, flipped(bits[i]))
        return copy(probe_part.at[2 + i], probe_got.at[1 + i], device, 12 * rounds + 1 + i)

    order = [(rel, j) for j in range(rounds) for rel in (1, 0)]
    for item in order[:2]:
        hop_in(*item).start()
    for j in range(rounds):
        own_swap(j).start()
    for local in loads[:3]:
        local.wait()
    row = lax.broadcasted_iota(jnp.int32, (arrays, half, size), 1)
    near_tile = tile + 1 - 2 * odd

    def merge(i):
        rel, j = order[i]
        hop_in(rel, j).wait_send()
        if i + 2 < len(order):
            hop_in(*order[i + 2]).start()
        hop_in(rel, j).wait_recv()
        slot = 2 * j + (1 - depth if rel else depth)
        begin = near_place[0, slot] - (near_tile - 1) * half
        near_rows = (row >= begin).astype(jnp.int32) != odd
        merged[rel, j] = jnp.where(near_rows, near_in[rel, j], hopped[rel, j])
        cross_in(rel, j).start()

    def pass_on(j):
        cross_in(1, j).wait_recv()
        rim_swap(j).start()

    def times(a, b):
        return a[0] * b[0] - a[1] * b[1], a[0] * b[1] + a[1] * b[0]

    def load(ref, s):
        return ref[s, 0], ref[s, 1]

    def apply(wave, right, left):
        return two_sided(wave[0], wave[1], right, left, pair, size)

    def rows(i):
        return slice(i * size, (i + 1) * size)

    def waves(p):
        spots = []
        for i in range(pair):
            j = p * pair + i
            slot = 2 * j + depth
            down = own_rows[slot] - (tile - 1) * half
            across = lax.rem(own_cols[slot], LANES)
            spots.append((j, slot, down, across, slot < filled))
            for part in range(2):
                psi[0, part, rows(i), :] = pltpu.roll(pltpu.roll(probe[part], down, 0), across, 1)
        for i in range(pair):
            j = spots[i][0]
            cross_in(0, j).wait_recv()
            own_swap(j).wait_recv()
            rim_swap(j).wait_recv()
            for s in range(slices):
                side = lax.rem(depth + s // group, 2)
                for part in range(2):
                    a = part * group + s % group
                    patch[s, part, i * size : i * size + half, :] = rim_in[side, j, a]
                    patch[s, part, i * size + half : (i + 1) * size, :] = own_in[side, j, a]
        for s in range(slices - 1):
            wave = apply(times(load(patch, s), load(psi, s)), a_right, a_left)
            psi[s + 1, 0] = wave[0]
            psi[s + 1, 1] = wave[1]
            yield
        s = slices - 1
        far = apply(times(load(patch, s), load(psi, s)), f_right, f_left)
        measured = jnp.concatenate([diff[spot[1]] for spot in spots], axis=0)
        misfit = far[0] * far[0] + far[1] * far[1] - measured
        hold[0] = misfit * far[0]
        hold[1] = -(misfit * far[1])
        yield
        for s in reversed(range(slices)):
            tabs = (f_right, f_left) if s == slices - 1 else (a_right, a_left)
            along = apply((hold[0], hold[1]), *tabs)
            term = times(load(psi, s), along)
            term = (term[0], -term[1])
            side = lax.rem(depth + s // group, 2)
            for i, (j, _, _, _, on) in enumerate(spots):
                for part in range(2):
                    a = part * group + s % group
                    value = jnp.where(on, term[part][rows(i)], 0.0)
                    rim_grad[side, j, a] = value[:half]
                    own_grad[side, j, a] = value[half:]
            back = times(load(patch, s), along)
            hold[0] = back[0]
            hold[1] = back[1]
            if s:
                yield
        for i in range(pair):
            j = spots[i][0]
            rim_return(j).start()
            own_return(j).start()
        yield
        for part in range(2):
            total = jnp.zeros((size, size), jnp.float32)
            for i, (_, _, down, across, on) in enumerate(spots):
                value = jnp.where(on, hold[part, rows(i), :], 0.0)
                value = pltpu.roll(value, lax.rem(size - down, size), 0)
                total = total + pltpu.roll(value, lax.rem(size - across, size), 1)
            total = total if part == 0 else -total
            for side in range(2):
                value = total[side * half : (side + 1) * half]
                if p:
                    value = value + probe_part[side, part]
                probe_part[side, part] = value

    first = waves(0)
    for i in range(len(order)):
        merge(i)
        if i == 4:
            pass_on(0)
            pass_on(1)
            for local in loads[3:]:
                local.wait()
        if i >= 5:
            next(first)
            next(first)
    pass_on(2)
    pass_on(3)
    next(first)
    next(first)

    back_order = [(0, 0), (0, 1), (1, 0), (1, 1), (0, 2), (0, 3), (1, 2), (1, 3)]

    def send_back(i):
        if i < len(back_order):
            rel, j = back_order[i]
            if rel:
                rim_return(j).wait_recv()
            cross_out(rel, j).start()

    def onto(i):
        cross_out(*back_order[i]).wait_send()
        send_back(i + 2)
        cross_out(*back_order[i]).wait_recv()
        hop_out(*back_order[i]).start()

    send_back(0)
    send_back(1)
    next(first, None)
    second = waves(1)
    for i in range(5):
        next(second)
    onto(0)
    next(second)
    onto(1)
    next(second)
    next(second)
    onto(2)
    next(second, None)

    probe_swap().start()

    probe_swap().wait_recv()
    probe_part[2] = probe_part[depth] + probe_got[0]
    probe_step(0).start()

    done = 0
    for i in range(3, len(back_order)):
        onto(i)
        if done < len(bits) - 1:
            probe_step(done).wait_recv()
            probe_part[3 + done] = probe_part[2 + done] + probe_got[1 + done]
            done += 1
            probe_step(done).start()
    while done < len(bits):
        probe_step(done).wait_recv()
        probe_part[3 + done] = probe_part[2 + done] + probe_got[1 + done]
        done += 1
        if done < len(bits):
            probe_step(done).start()
    probe_out[...] = probe_part[2 + len(bits)]
    own_k_out[...] = own_grad[0]

    def drain(j, carry):
        own_return(j).wait_recv()
        for rel in range(2):
            hop_out(rel, j).wait_recv()
            hop_out(rel, j).wait_send()
            cross_in(rel, j).wait_send()
        own_swap(j).wait_send()
        rim_swap(j).wait_send()
        own_return(j).wait_send()
        rim_return(j).wait_send()
        return carry

    lax.fori_loop(0, rounds, drain, 0)
    probe_swap().wait_send()
    for i in range(len(bits)):
        probe_step(i).wait_send()


def scatter_kernel(own_cols, near_place, far_place, own_k, own_g, near_k, near_g, far_k, far_g, out):
    depth, tile, odd = axis_places()
    blocks = out.shape[2] // LANES
    shape = (out.shape[0], out.shape[1], LANES)
    lane = lax.broadcasted_iota(jnp.int32, shape, 2)
    row = lax.broadcasted_iota(jnp.int32, shape, 1)
    out[...] = jnp.zeros_like(out)
    for index, ref in enumerate((own_k, own_g, near_k, near_g, far_k, far_g)):
        which, rel = index // 2, index % 2

        def one(j, carry, which=which, rel=rel, ref=ref):
            slot = 2 * j + (depth if rel == 0 else 1 - depth)
            value = ref[j]
            col = own_cols[slot] if which == 0 else (near_place, far_place)[which - 1][1, slot]
            if which:
                under = odd if which == 1 else 1 - odd
                place = (near_place, far_place)[which - 1]
                owner = tile + (1 - 2 * odd if which == 1 else 2 * odd - 1)
                start = place[0, slot] - (owner - 1) * shape[1]
                low = jnp.where(under == 1, 0, start)
                high = jnp.where(under == 1, start, shape[1])
                exists = (owner >= 0) & (owner < lax.axis_size("tile"))
                high = jnp.where(exists, high, low)
                value = jnp.where((row >= low) & (row < high), value, 0.0)
            block = col // LANES
            after = jnp.minimum(block + 1, blocks - 1)
            inside = lane >= col - block * LANES
            at = pl.ds(pl.multiple_of(block * LANES, LANES), LANES)
            out[:, :, at] = out[:, :, at] + jnp.where(inside, value, 0.0)
            at = pl.ds(pl.multiple_of(after * LANES, LANES), LANES)
            out[:, :, at] = out[:, :, at] + jnp.where(inside, 0.0, value)
            return carry

        lax.fori_loop(0, ref.shape[0], one, 0)


SMEM = pl.BlockSpec(memory_space=pltpu.SMEM)
VMEM = pl.BlockSpec(memory_space=pltpu.VMEM)
ANY = pl.BlockSpec(memory_space=pl.ANY)
PARAMS = pltpu.CompilerParams(vmem_limit_bytes=48 * 1024 * 1024)


def shards(transmission, probe, scan_rows, scan_cols, tile_counts, diffraction):
    size = probe.shape[-1]
    half = size // 2
    group, strip, cols = transmission.shape[1:]
    rounds = scan_rows.shape[0] // 2
    tiles = lax.axis_size("tile")
    f32 = jnp.float32

    beside = [(c, c ^ 1) for c in range(tiles)]
    across = [(c, c + 1 if c % 2 else c - 1) for c in range(1, tiles - 1)]

    place = jnp.stack([scan_rows, scan_cols])
    place_near = lax.ppermute(place, "tile", beside)
    place_far = lax.ppermute(place, "tile", across)

    flat = transmission.reshape(2 * group, strip, cols)
    piece = jax.ShapeDtypeStruct((rounds, 2 * group, strip, LANES), f32)
    own_k, own_g, near_k, near_g, far_k, far_g = pl.pallas_call(
        gather_kernel,
        out_shape=[piece] * 6,
        in_specs=[SMEM] * 3 + [VMEM],
        out_specs=[VMEM] * 6,
        compiler_params=PARAMS,
        name="gather",
    )(scan_cols, place_near, place_far, flat)

    tabs = [jnp.asarray(t) for t in tables(size)]
    pair = 2
    stages = (tiles - 1).bit_length()
    sems = pltpu.SemaphoreType.DMA((12 * rounds + 1 + stages,))
    both = pltpu.VMEM((2,) + piece.shape, f32)
    single = pltpu.VMEM(piece.shape, f32)
    waves = pltpu.VMEM((2 * group, 2, pair * size, size), f32)
    rows_shape = (probe.shape[0], half, size)
    *parts, probe_grad = pl.pallas_call(
        main_kernel,
        out_shape=[piece] * 6 + [jax.ShapeDtypeStruct(rows_shape, f32)],
        in_specs=[SMEM] * 4 + [ANY] * 12,
        out_specs=[VMEM] * 7,
        scratch_shapes=[both, both, both, single, single, both, both, both, both]
        + [waves, waves, pltpu.VMEM((2, pair * size, size), f32)]
        + [pltpu.VMEM((3 + stages,) + rows_shape, f32), pltpu.VMEM((1 + stages,) + rows_shape, f32)]
        + [pltpu.VMEM(probe.shape, f32), pltpu.VMEM(diffraction.shape, f32)]
        + [pltpu.VMEM(t.shape, t.dtype) for t in tabs]
        + [sems, sems, pltpu.SemaphoreType.DMA((9,))],
        compiler_params=pltpu.CompilerParams(
            vmem_limit_bytes=48 * 1024 * 1024, collective_id=0, has_side_effects=True
        ),
        name="waves",
    )(
        scan_rows, scan_cols, tile_counts, place_near, probe, diffraction,
        own_k, own_g, near_k, near_g, far_k, far_g, *tabs,
    )

    grads = pl.pallas_call(
        scatter_kernel,
        out_shape=jax.ShapeDtypeStruct(flat.shape, f32),
        in_specs=[SMEM] * 3 + [VMEM] * 6,
        out_specs=VMEM,
        compiler_params=PARAMS,
        name="scatter",
    )(scan_cols, place_near, place_far, *parts)
    return (grads.reshape(transmission.shape), probe_grad)


def solution(mesh):
    placed = (P(None, "depth", "tile", None), P(), P("tile"), P("tile"), P(), P("tile", None, None))
    return jax.shard_map(
        shards,
        mesh=mesh,
        in_specs=placed,
        out_specs=(P(None, "depth", "tile", None), P(None, "depth", None)),
        check_vma=False,
    )
```

```python
import math

import jax
import jax.numpy as jnp
import ml_dtypes
import numpy as np
from jax import lax
from jax.experimental import pallas as pl
from jax.experimental.pallas import tpu as pltpu
from jax.sharding import PartitionSpec as P

FRESNEL = 0.5
LANES = 128


def split_table(table):
    head = table.astype(np.float32).astype(ml_dtypes.bfloat16)
    tail = (table - head.astype(np.float64)).astype(np.float32).astype(ml_dtypes.bfloat16)
    return np.concatenate([head, tail])


def tables(size):
    index = np.arange(size)
    dft = np.exp(-2j * math.pi / size * (index[:, None] * index[None, :] % size)) / math.sqrt(size)
    freq = (index + size // 2) % size - size // 2
    phase = np.exp(-1j * FRESNEL * math.pi / size * freq.astype(np.float64) ** 2)
    prop = dft.conj() @ (phase[:, None] * dft)
    prop = 0.5 * (prop + prop.T)
    out = []
    for m in (prop, dft):
        right = np.block([[m.real, m.imag], [-m.imag, m.real]])
        out += [split_table(right), split_table(right.T)]
    return out


def halves(x):
    head = x.astype(jnp.bfloat16)
    tail = (x - head.astype(jnp.float32)).astype(jnp.bfloat16)
    return head, tail


def dot(a, b):
    return jnp.dot(a, b, preferred_element_type=jnp.float32)


def two_sided(re, im, right, left, slots, size):
    count = slots * size
    head, tail = halves(jnp.concatenate([re, im], axis=1))
    y = dot(jnp.concatenate([head, tail], axis=0), right[: 2 * size])
    y = y[:count] + y[count:] + dot(head, right[2 * size :])
    z = jnp.concatenate(
        [
            jnp.concatenate(
                [y[j * size : (j + 1) * size, :size], y[j * size : (j + 1) * size, size:]], axis=0
            )
            for j in range(slots)
        ],
        axis=1,
    )
    head, tail = halves(z)
    y = dot(left[...], head)
    y = y[: 2 * size] + y[2 * size :] + dot(left[: 2 * size], tail)
    out_re = [y[:size, j * size : (j + 1) * size] for j in range(slots)]
    out_im = [y[size:, j * size : (j + 1) * size] for j in range(slots)]
    return jnp.concatenate(out_re, axis=0), jnp.concatenate(out_im, axis=0)


def axis_places():
    depth = lax.axis_index("depth")
    tile = lax.axis_index("tile")
    return depth, tile, lax.rem(tile, 2)


def gather_kernel(own_cols, near_place, far_place, trans, *outs):
    depth, _, _ = axis_places()
    blocks = trans.shape[2] // LANES
    shape = (trans.shape[0], trans.shape[1], LANES)
    lane = lax.broadcasted_iota(jnp.int32, shape, 2)
    for which in range(3):
        for rel in range(2):
            out = outs[2 * which + rel]

            def one(j, carry, which=which, rel=rel, out=out):
                slot = 2 * j + (depth if rel == 0 else 1 - depth)
                col = own_cols[slot] if which == 0 else (near_place, far_place)[which - 1][1, slot]
                block = col // LANES
                after = jnp.minimum(block + 1, blocks - 1)
                x = trans[:, :, pl.ds(pl.multiple_of(block * LANES, LANES), LANES)]
                y = trans[:, :, pl.ds(pl.multiple_of(after * LANES, LANES), LANES)]
                out[j] = jnp.where(lane >= col - block * LANES, x, y)
                return carry

            lax.fori_loop(0, out.shape[0], one, 0)


MESH = pl.DeviceIdType.MESH
WINDOW = 3


def main_kernel(
    own_rows, own_cols, counts, near_place, probe_hbm, diff_hbm,
    own_k, own_g, near_k, near_g, far_k, far_g, *rest,
):
    tables_hbm, rest = rest[:4], rest[4:]
    exchange(
        own_rows, own_cols, counts, near_place, probe_hbm, diff_hbm,
        own_k, own_g, near_k, near_g, far_k, far_g, tables_hbm, *rest,
    )


def exchange(
    own_rows, own_cols, counts, near_place, probe_hbm, diff_hbm,
    own_k, own_g, near_k, near_g, far_k, far_g, tables_hbm,
    own_k_out, own_g_out, near_k_out, near_g_out, far_k_out, far_g_out, probe_out,
    hopped, merged, rim_in, give_in, rim_back, own_in, near_in, rim_grad, own_grad, patch, psi, hold,
    probe_part, probe_got, probe, diff, a_right, a_left, f_right, f_left,
    send_sem, recv_sem, load_sem,
):
    depth, tile, odd = axis_places()
    tiles = lax.axis_size("tile")
    filled = counts[tile]
    rounds, arrays, half, size = own_k.shape
    group = arrays // 2
    slices = 2 * group
    pair = patch.shape[2] // size

    def flipped(bit):
        return tile + bit - 2 * bit * lax.rem(lax.div(tile, bit), 2)

    other = (1 - depth, tile)
    beside = (depth, flipped(1))
    onward = (depth, lax.rem(tile + 4 * odd - 2 + tiles, tiles))
    backward = (depth, lax.rem(tile - 4 * odd + 2 + tiles, tiles))
    bits = []
    while 2 ** len(bits) < tiles:
        bits.append(2 ** len(bits))
    bits = bits[::-1]

    loads = [
        pltpu.make_async_copy(src, dst, load_sem.at[i])
        for i, (src, dst) in enumerate(
            (
                (near_g, near_in.at[1]),
                (near_k, near_in.at[0]),
                (own_k, own_in.at[0]),
                (probe_hbm, probe),
                (diff_hbm, diff),
                *zip(tables_hbm, (a_right, a_left, f_right, f_left)),
            )
        )
    ]
    for local in loads:
        local.start()
    barrier = pltpu.get_barrier_semaphore()
    greeted = [other, beside, onward, backward] + [(depth, flipped(b)) for b in bits if b > 2]
    for device in greeted:
        pl.semaphore_signal(barrier, inc=1, device_id=device, device_id_type=MESH)
    pl.semaphore_wait(barrier, len(greeted))

    def copy(src, dst, device, sem):
        return pltpu.make_async_remote_copy(
            src_ref=src, dst_ref=dst, send_sem=send_sem.at[sem], recv_sem=recv_sem.at[sem],
            device_id=device, device_id_type=MESH,
        )

    def hop_in(rel, j):
        return copy((far_k, far_g)[rel].at[j], hopped.at[rel, j], onward, rel * rounds + j)

    def cross_in(rel, j):
        dst = give_in.at[j] if rel else rim_in.at[0, j]
        return copy(merged.at[rel, j], dst, beside, (2 + rel) * rounds + j)

    def own_swap(j):
        return copy(own_g.at[j], own_in.at[1, j], other, 4 * rounds + j)

    def rim_swap(j):
        return copy(give_in.at[j], rim_in.at[1, j], other, 5 * rounds + j)

    def own_return(j):
        return copy(own_grad.at[1, j], own_g_out.at[j], other, 6 * rounds + j)

    def rim_return(j):
        return copy(rim_grad.at[1, j], rim_back.at[j], other, 7 * rounds + j)

    def cross_out(rel, j):
        src = rim_back.at[j] if rel else rim_grad.at[0, j]
        return copy(src, (near_k_out, near_g_out)[rel].at[j], beside, (8 + rel) * rounds + j)

    def hop_out(rel, j):
        refs = ((near_k_out, far_k_out), (near_g_out, far_g_out))[rel]
        return copy(refs[0].at[j], refs[1].at[j], backward, (10 + rel) * rounds + j)

    def probe_swap():
        return copy(probe_part.at[1 - depth], probe_got.at[0], other, 12 * rounds)

    def probe_step(i):
        device = (depth, flipped(bits[i]))
        return copy(probe_part.at[2 + i], probe_got.at[1 + i], device, 12 * rounds + 1 + i)

    order = [(rel, j) for j in range(rounds) for rel in (1, 0)]
    for item in order[:WINDOW]:
        hop_in(*item).start()
    for j in range(rounds):
        own_swap(j).start()
    for local in loads[:3]:
        local.wait()
    row = lax.broadcasted_iota(jnp.int32, (arrays, half, size), 1)
    near_tile = tile + 1 - 2 * odd

    def merge(i):
        rel, j = order[i]
        hop_in(rel, j).wait_send()
        if i + WINDOW < len(order):
            hop_in(*order[i + WINDOW]).start()
        hop_in(rel, j).wait_recv()
        slot = 2 * j + (1 - depth if rel else depth)
        begin = near_place[0, slot] - (near_tile - 1) * half
        near_rows = (row >= begin).astype(jnp.int32) != odd
        merged[rel, j] = jnp.where(near_rows, near_in[rel, j], hopped[rel, j])
        cross_in(rel, j).start()

    def pass_on(j):
        cross_in(1, j).wait_recv()
        rim_swap(j).start()

    def times(a, b):
        return a[0] * b[0] - a[1] * b[1], a[0] * b[1] + a[1] * b[0]

    def load(ref, s):
        return ref[s, 0], ref[s, 1]

    def apply(wave, right, left):
        return two_sided(wave[0], wave[1], right, left, pair, size)

    def rows(i):
        return slice(i * size, (i + 1) * size)

    def waves(p):
        spots = []
        for i in range(pair):
            j = p * pair + i
            slot = 2 * j + depth
            down = own_rows[slot] - (tile - 1) * half
            across = lax.rem(own_cols[slot], LANES)
            spots.append((j, slot, down, across, slot < filled))
            for part in range(2):
                psi[0, part, rows(i), :] = pltpu.roll(pltpu.roll(probe[part], down, 0), across, 1)
        for i in range(pair):
            j = spots[i][0]
            cross_in(0, j).wait_recv()
            own_swap(j).wait_recv()
            rim_swap(j).wait_recv()
            for s in range(slices):
                side = lax.rem(depth + s // group, 2)
                for part in range(2):
                    a = part * group + s % group
                    patch[s, part, i * size : i * size + half, :] = rim_in[side, j, a]
                    patch[s, part, i * size + half : (i + 1) * size, :] = own_in[side, j, a]
        for s in range(slices - 1):
            wave = apply(times(load(patch, s), load(psi, s)), a_right, a_left)
            psi[s + 1, 0] = wave[0]
            psi[s + 1, 1] = wave[1]
            yield
        s = slices - 1
        far = apply(times(load(patch, s), load(psi, s)), f_right, f_left)
        measured = jnp.concatenate([diff[spot[1]] for spot in spots], axis=0)
        misfit = far[0] * far[0] + far[1] * far[1] - measured
        hold[0] = misfit * far[0]
        hold[1] = -(misfit * far[1])
        yield
        for s in reversed(range(slices)):
            tabs = (f_right, f_left) if s == slices - 1 else (a_right, a_left)
            along = apply((hold[0], hold[1]), *tabs)
            term = times(load(psi, s), along)
            term = (term[0], -term[1])
            side = lax.rem(depth + s // group, 2)
            for i, (j, _, _, _, on) in enumerate(spots):
                for part in range(2):
                    a = part * group + s % group
                    value = jnp.where(on, term[part][rows(i)], 0.0)
                    rim_grad[side, j, a] = value[:half]
                    own_grad[side, j, a] = value[half:]
            back = times(load(patch, s), along)
            hold[0] = back[0]
            hold[1] = back[1]
            if s:
                yield
        for i in range(pair):
            j = spots[i][0]
            rim_return(j).start()
            own_return(j).start()
        yield
        for part in range(2):
            total = jnp.zeros((size, size), jnp.float32)
            for i, (_, _, down, across, on) in enumerate(spots):
                value = jnp.where(on, hold[part, rows(i), :], 0.0)
                value = pltpu.roll(value, lax.rem(size - down, size), 0)
                total = total + pltpu.roll(value, lax.rem(size - across, size), 1)
            total = total if part == 0 else -total
            for side in range(2):
                value = total[side * half : (side + 1) * half]
                if p:
                    value = value + probe_part[side, part]
                probe_part[side, part] = value

    first = waves(0)
    for i in range(len(order)):
        merge(i)
        if i == 4:
            pass_on(0)
            pass_on(1)
            for local in loads[3:]:
                local.wait()
        if i >= 5:
            next(first)
            next(first)
    pass_on(2)
    pass_on(3)
    next(first)
    next(first)

    back_order = [(0, 0), (0, 1), (1, 0), (1, 1), (0, 2), (0, 3), (1, 2), (1, 3)]

    def send_back(i):
        if i < len(back_order):
            rel, j = back_order[i]
            if rel:
                rim_return(j).wait_recv()
            cross_out(rel, j).start()

    def onto(i):
        cross_out(*back_order[i]).wait_send()
        send_back(i + WINDOW)
        cross_out(*back_order[i]).wait_recv()
        hop_out(*back_order[i]).start()

    send_back(0)
    send_back(1)
    next(first, None)
    send_back(2)
    second = waves(1)
    for i in range(5):
        next(second)
    onto(0)
    next(second)
    next(second)
    next(second)
    onto(1)
    onto(2)
    next(second, None)

    probe_swap().start()

    probe_swap().wait_recv()
    probe_part[2] = probe_part[depth] + probe_got[0]
    probe_step(0).start()

    done = 0
    for i in range(3, len(back_order)):
        onto(i)
        if done < len(bits) - 1:
            probe_step(done).wait_recv()
            probe_part[3 + done] = probe_part[2 + done] + probe_got[1 + done]
            done += 1
            probe_step(done).start()
    while done < len(bits):
        probe_step(done).wait_recv()
        probe_part[3 + done] = probe_part[2 + done] + probe_got[1 + done]
        done += 1
        if done < len(bits):
            probe_step(done).start()
    probe_out[...] = probe_part[2 + len(bits)]
    own_k_out[...] = own_grad[0]

    def drain(j, carry):
        own_return(j).wait_recv()
        for rel in range(2):
            hop_out(rel, j).wait_recv()
            hop_out(rel, j).wait_send()
            cross_in(rel, j).wait_send()
        own_swap(j).wait_send()
        rim_swap(j).wait_send()
        own_return(j).wait_send()
        rim_return(j).wait_send()
        return carry

    lax.fori_loop(0, rounds, drain, 0)
    probe_swap().wait_send()
    for i in range(len(bits)):
        probe_step(i).wait_send()


def scatter_kernel(own_cols, near_place, far_place, own_k, own_g, near_k, near_g, far_k, far_g, out):
    depth, tile, odd = axis_places()
    blocks = out.shape[2] // LANES
    shape = (out.shape[0], out.shape[1], LANES)
    lane = lax.broadcasted_iota(jnp.int32, shape, 2)
    row = lax.broadcasted_iota(jnp.int32, shape, 1)
    out[...] = jnp.zeros_like(out)
    for index, ref in enumerate((own_k, own_g, near_k, near_g, far_k, far_g)):
        which, rel = index // 2, index % 2

        def one(j, carry, which=which, rel=rel, ref=ref):
            slot = 2 * j + (depth if rel == 0 else 1 - depth)
            value = ref[j]
            col = own_cols[slot] if which == 0 else (near_place, far_place)[which - 1][1, slot]
            if which:
                under = odd if which == 1 else 1 - odd
                place = (near_place, far_place)[which - 1]
                owner = tile + (1 - 2 * odd if which == 1 else 2 * odd - 1)
                start = place[0, slot] - (owner - 1) * shape[1]
                low = jnp.where(under == 1, 0, start)
                high = jnp.where(under == 1, start, shape[1])
                exists = (owner >= 0) & (owner < lax.axis_size("tile"))
                high = jnp.where(exists, high, low)
                value = jnp.where((row >= low) & (row < high), value, 0.0)
            block = col // LANES
            after = jnp.minimum(block + 1, blocks - 1)
            inside = lane >= col - block * LANES
            at = pl.ds(pl.multiple_of(block * LANES, LANES), LANES)
            out[:, :, at] = out[:, :, at] + jnp.where(inside, value, 0.0)
            at = pl.ds(pl.multiple_of(after * LANES, LANES), LANES)
            out[:, :, at] = out[:, :, at] + jnp.where(inside, 0.0, value)
            return carry

        lax.fori_loop(0, ref.shape[0], one, 0)


SMEM = pl.BlockSpec(memory_space=pltpu.SMEM)
VMEM = pl.BlockSpec(memory_space=pltpu.VMEM)
ANY = pl.BlockSpec(memory_space=pl.ANY)
PARAMS = pltpu.CompilerParams(vmem_limit_bytes=16 * 1024 * 1024)


def shards(transmission, probe, scan_rows, scan_cols, tile_counts, diffraction):
    size = probe.shape[-1]
    half = size // 2
    group, strip, cols = transmission.shape[1:]
    rounds = scan_rows.shape[0] // 2
    tiles = lax.axis_size("tile")
    f32 = jnp.float32

    beside = [(c, c ^ 1) for c in range(tiles)]
    across = [(c, c + 1 if c % 2 else c - 1) for c in range(1, tiles - 1)]

    place = jnp.stack([scan_rows, scan_cols])
    place_near = lax.ppermute(place, "tile", beside)
    place_far = lax.ppermute(place, "tile", across)

    flat = transmission.reshape(2 * group, strip, cols)
    piece = jax.ShapeDtypeStruct((rounds, 2 * group, strip, LANES), f32)
    own_k, own_g, near_k, near_g, far_k, far_g = pl.pallas_call(
        gather_kernel,
        out_shape=[piece] * 6,
        in_specs=[SMEM] * 3 + [VMEM],
        out_specs=[VMEM] * 6,
        compiler_params=PARAMS,
        name="gather",
    )(scan_cols, place_near, place_far, flat)

    tabs = [jnp.asarray(t) for t in tables(size)]
    pair = 2
    stages = (tiles - 1).bit_length()
    sems = pltpu.SemaphoreType.DMA((12 * rounds + 1 + stages,))
    both = pltpu.VMEM((2,) + piece.shape, f32)
    single = pltpu.VMEM(piece.shape, f32)
    waves = pltpu.VMEM((2 * group, 2, pair * size, size), f32)
    rows_shape = (probe.shape[0], half, size)
    *parts, probe_grad = pl.pallas_call(
        main_kernel,
        out_shape=[piece] * 6 + [jax.ShapeDtypeStruct(rows_shape, f32)],
        in_specs=[SMEM] * 4 + [ANY] * 12,
        out_specs=[VMEM] * 7,
        scratch_shapes=[both, both, both, single, single, both, both, both, both]
        + [waves, waves, pltpu.VMEM((2, pair * size, size), f32)]
        + [pltpu.VMEM((3 + stages,) + rows_shape, f32), pltpu.VMEM((1 + stages,) + rows_shape, f32)]
        + [pltpu.VMEM(probe.shape, f32), pltpu.VMEM(diffraction.shape, f32)]
        + [pltpu.VMEM(t.shape, t.dtype) for t in tabs]
        + [sems, sems, pltpu.SemaphoreType.DMA((9,))],
        compiler_params=pltpu.CompilerParams(
            vmem_limit_bytes=24 * 1024 * 1024, collective_id=0, has_side_effects=True
        ),
        name="waves",
    )(
        scan_rows, scan_cols, tile_counts, place_near, probe, diffraction,
        own_k, own_g, near_k, near_g, far_k, far_g, *tabs,
    )

    grads = pl.pallas_call(
        scatter_kernel,
        out_shape=jax.ShapeDtypeStruct(flat.shape, f32),
        in_specs=[SMEM] * 3 + [VMEM] * 6,
        out_specs=VMEM,
        compiler_params=PARAMS,
        name="scatter",
    )(scan_cols, place_near, place_far, *parts)
    return (grads.reshape(transmission.shape), probe_grad)


def solution(mesh):
    placed = (P(None, "depth", "tile", None), P(), P("tile"), P("tile"), P(), P("tile", None, None))
    return jax.shard_map(
        shards,
        mesh=mesh,
        in_specs=placed,
        out_specs=(P(None, "depth", "tile", None), P(None, "depth", None)),
        check_vma=False,
    )
```

```python
import math

import jax
import jax.numpy as jnp
import ml_dtypes
import numpy as np
from jax import lax
from jax.experimental import pallas as pl
from jax.experimental.pallas import tpu as pltpu
from jax.sharding import PartitionSpec as P

FRESNEL = 0.5
LANES = 128


def split_table(table):
    head = table.astype(np.float32).astype(ml_dtypes.bfloat16)
    tail = (table - head.astype(np.float64)).astype(np.float32).astype(ml_dtypes.bfloat16)
    return np.concatenate([head, tail])


def tables(size):
    index = np.arange(size)
    dft = np.exp(-2j * math.pi / size * (index[:, None] * index[None, :] % size)) / math.sqrt(size)
    freq = (index + size // 2) % size - size // 2
    phase = np.exp(-1j * FRESNEL * math.pi / size * freq.astype(np.float64) ** 2)
    prop = dft.conj() @ (phase[:, None] * dft)
    prop = 0.5 * (prop + prop.T)
    out = []
    for m in (prop, dft):
        right = np.block([[m.real, m.imag], [-m.imag, m.real]])
        out += [split_table(right), split_table(right.T)]
    return out


def halves(x):
    head = x.astype(jnp.bfloat16)
    tail = (x - head.astype(jnp.float32)).astype(jnp.bfloat16)
    return head, tail


def dot(a, b):
    return jnp.dot(a, b, preferred_element_type=jnp.float32)


def two_sided(re, im, right, left, slots, size):
    count = slots * size
    head, tail = halves(jnp.concatenate([re, im], axis=1))
    y = dot(jnp.concatenate([head, tail], axis=0), right[: 2 * size])
    y = y[:count] + y[count:] + dot(head, right[2 * size :])
    z = jnp.concatenate(
        [
            jnp.concatenate(
                [y[j * size : (j + 1) * size, :size], y[j * size : (j + 1) * size, size:]], axis=0
            )
            for j in range(slots)
        ],
        axis=1,
    )
    head, tail = halves(z)
    y = dot(left[...], head)
    y = y[: 2 * size] + y[2 * size :] + dot(left[: 2 * size], tail)
    out_re = [y[:size, j * size : (j + 1) * size] for j in range(slots)]
    out_im = [y[size:, j * size : (j + 1) * size] for j in range(slots)]
    return jnp.concatenate(out_re, axis=0), jnp.concatenate(out_im, axis=0)


def axis_places():
    depth = lax.axis_index("depth")
    tile = lax.axis_index("tile")
    return depth, tile, lax.rem(tile, 2)


def gather_kernel(own_cols, near_place, far_place, trans, *outs):
    depth, _, _ = axis_places()
    blocks = trans.shape[2] // LANES
    shape = (trans.shape[0], trans.shape[1], LANES)
    lane = lax.broadcasted_iota(jnp.int32, shape, 2)
    for which in range(3):
        for rel in range(2):
            out = outs[2 * which + rel]

            def one(j, carry, which=which, rel=rel, out=out):
                slot = 2 * j + (depth if rel == 0 else 1 - depth)
                col = own_cols[slot] if which == 0 else (near_place, far_place)[which - 1][1, slot]
                block = col // LANES
                after = jnp.minimum(block + 1, blocks - 1)
                x = trans[:, :, pl.ds(pl.multiple_of(block * LANES, LANES), LANES)]
                y = trans[:, :, pl.ds(pl.multiple_of(after * LANES, LANES), LANES)]
                out[j] = jnp.where(lane >= col - block * LANES, x, y)
                return carry

            lax.fori_loop(0, out.shape[0], one, 0)


MESH = pl.DeviceIdType.MESH
WINDOW = 3


def main_kernel(
    own_rows, own_cols, counts, near_place, probe_hbm, diff_hbm,
    own_k, own_g, near_k, near_g, far_k, far_g, *rest,
):
    tables_hbm, rest = rest[:4], rest[4:]
    exchange(
        own_rows, own_cols, counts, near_place, probe_hbm, diff_hbm,
        own_k, own_g, near_k, near_g, far_k, far_g, tables_hbm, *rest,
    )


def exchange(
    own_rows, own_cols, counts, near_place, probe_hbm, diff_hbm,
    own_k, own_g, near_k, near_g, far_k, far_g, tables_hbm,
    own_k_out, own_g_out, near_k_out, near_g_out, far_k_out, far_g_out, probe_out,
    hopped, merged, rim_in, give_in, rim_back, own_in, near_in, rim_grad, own_grad, patch, psi, hold,
    probe_part, probe_got, probe, diff, a_right, a_left, f_right, f_left,
    send_sem, recv_sem, load_sem,
):
    depth, tile, odd = axis_places()
    tiles = lax.axis_size("tile")
    filled = counts[tile]
    rounds, arrays, half, size = own_k.shape
    group = arrays // 2
    slices = 2 * group
    pair = patch.shape[2] // size

    def flipped(bit):
        return tile + bit - 2 * bit * lax.rem(lax.div(tile, bit), 2)

    other = (1 - depth, tile)
    beside = (depth, flipped(1))
    onward = (depth, lax.rem(tile + 4 * odd - 2 + tiles, tiles))
    backward = (depth, lax.rem(tile - 4 * odd + 2 + tiles, tiles))
    bits = []
    while 2 ** len(bits) < tiles:
        bits.append(2 ** len(bits))
    bits = bits[::-1]

    loads = [
        pltpu.make_async_copy(src, dst, load_sem.at[i])
        for i, (src, dst) in enumerate(
            (
                (near_g, near_in.at[1]),
                (near_k, near_in.at[0]),
                (own_k, own_in.at[0]),
                (probe_hbm, probe),
                (diff_hbm, diff),
                *zip(tables_hbm, (a_right, a_left, f_right, f_left)),
            )
        )
    ]
    for local in loads:
        local.start()
    barrier = pltpu.get_barrier_semaphore()
    greeted = [other, beside, onward, backward] + [(depth, flipped(b)) for b in bits if b > 2]
    for device in greeted:
        pl.semaphore_signal(barrier, inc=1, device_id=device, device_id_type=MESH)
    pl.semaphore_wait(barrier, len(greeted))

    def copy(src, dst, device, sem):
        return pltpu.make_async_remote_copy(
            src_ref=src, dst_ref=dst, send_sem=send_sem.at[sem], recv_sem=recv_sem.at[sem],
            device_id=device, device_id_type=MESH,
        )

    def hop_in(rel, j):
        return copy((far_k, far_g)[rel].at[j], hopped.at[rel, j], onward, rel * rounds + j)

    def cross_in(rel, j):
        dst = give_in.at[j] if rel else rim_in.at[0, j]
        return copy(merged.at[rel, j], dst, beside, (2 + rel) * rounds + j)

    def own_swap(j):
        return copy(own_g.at[j], own_in.at[1, j], other, 4 * rounds + j)

    def rim_swap(j):
        return copy(give_in.at[j], rim_in.at[1, j], other, 5 * rounds + j)

    def own_return(j):
        return copy(own_grad.at[1, j], own_g_out.at[j], other, 6 * rounds + j)

    def rim_return(j):
        return copy(rim_grad.at[1, j], rim_back.at[j], other, 7 * rounds + j)

    def cross_out(rel, j):
        src = rim_back.at[j] if rel else rim_grad.at[0, j]
        return copy(src, (near_k_out, near_g_out)[rel].at[j], beside, (8 + rel) * rounds + j)

    def hop_out(rel, j):
        refs = ((near_k_out, far_k_out), (near_g_out, far_g_out))[rel]
        return copy(refs[0].at[j], refs[1].at[j], backward, (10 + rel) * rounds + j)

    def probe_swap():
        return copy(probe_part.at[1 - depth], probe_got.at[0], other, 12 * rounds)

    def probe_step(i):
        device = (depth, flipped(bits[i]))
        return copy(probe_part.at[2 + i], probe_got.at[1 + i], device, 12 * rounds + 1 + i)

    order = [(rel, j) for j in range(rounds) for rel in (1, 0)]
    for item in order[:WINDOW]:
        hop_in(*item).start()
    for j in range(rounds):
        own_swap(j).start()
    for local in loads[:3]:
        local.wait()
    row = lax.broadcasted_iota(jnp.int32, (arrays, half, size), 1)
    near_tile = tile + 1 - 2 * odd

    def merge(i):
        rel, j = order[i]
        hop_in(rel, j).wait_send()
        if i + WINDOW < len(order):
            hop_in(*order[i + WINDOW]).start()
        hop_in(rel, j).wait_recv()
        slot = 2 * j + (1 - depth if rel else depth)
        begin = near_place[0, slot] - (near_tile - 1) * half
        near_rows = (row >= begin).astype(jnp.int32) != odd
        merged[rel, j] = jnp.where(near_rows, near_in[rel, j], hopped[rel, j])
        cross_in(rel, j).start()

    def pass_on(j):
        cross_in(1, j).wait_recv()
        rim_swap(j).start()

    def times(a, b):
        return a[0] * b[0] - a[1] * b[1], a[0] * b[1] + a[1] * b[0]

    def load(ref, s):
        return ref[s, 0], ref[s, 1]

    def apply(wave, right, left):
        return two_sided(wave[0], wave[1], right, left, pair, size)

    def rows(i):
        return slice(i * size, (i + 1) * size)

    def waves(p):
        spots = []
        for i in range(pair):
            j = p * pair + i
            slot = 2 * j + depth
            down = own_rows[slot] - (tile - 1) * half
            across = lax.rem(own_cols[slot], LANES)
            spots.append((j, slot, down, across, slot < filled))
            for part in range(2):
                psi[0, part, rows(i), :] = pltpu.roll(pltpu.roll(probe[part], down, 0), across, 1)
        for i in range(pair):
            j = spots[i][0]
            cross_in(0, j).wait_recv()
            own_swap(j).wait_recv()
            rim_swap(j).wait_recv()
            for s in range(slices):
                side = lax.rem(depth + s // group, 2)
                for part in range(2):
                    a = part * group + s % group
                    patch[s, part, i * size : i * size + half, :] = rim_in[side, j, a]
                    patch[s, part, i * size + half : (i + 1) * size, :] = own_in[side, j, a]
        for s in range(slices - 1):
            wave = apply(times(load(patch, s), load(psi, s)), a_right, a_left)
            psi[s + 1, 0] = wave[0]
            psi[s + 1, 1] = wave[1]
            yield
        s = slices - 1
        far = apply(times(load(patch, s), load(psi, s)), f_right, f_left)
        measured = jnp.concatenate([diff[spot[1]] for spot in spots], axis=0)
        misfit = far[0] * far[0] + far[1] * far[1] - measured
        hold[0] = misfit * far[0]
        hold[1] = -(misfit * far[1])
        yield
        for s in reversed(range(slices)):
            tabs = (f_right, f_left) if s == slices - 1 else (a_right, a_left)
            along = apply((hold[0], hold[1]), *tabs)
            term = times(load(psi, s), along)
            term = (term[0], -term[1])
            side = lax.rem(depth + s // group, 2)
            for i, (j, _, _, _, on) in enumerate(spots):
                for part in range(2):
                    a = part * group + s % group
                    value = jnp.where(on, term[part][rows(i)], 0.0)
                    rim_grad[side, j, a] = value[:half]
                    own_grad[side, j, a] = value[half:]
            back = times(load(patch, s), along)
            hold[0] = back[0]
            hold[1] = back[1]
            if s:
                yield
        for i in range(pair):
            j = spots[i][0]
            rim_return(j).start()
            own_return(j).start()
        yield
        for part in range(2):
            total = jnp.zeros((size, size), jnp.float32)
            for i, (_, _, down, across, on) in enumerate(spots):
                value = jnp.where(on, hold[part, rows(i), :], 0.0)
                value = pltpu.roll(value, lax.rem(size - down, size), 0)
                total = total + pltpu.roll(value, lax.rem(size - across, size), 1)
            total = total if part == 0 else -total
            for side in range(2):
                value = total[side * half : (side + 1) * half]
                if p:
                    value = value + probe_part[side, part]
                probe_part[side, part] = value

    first = waves(0)
    for i in range(len(order)):
        merge(i)
        if i == 4:
            pass_on(0)
            pass_on(1)
            for local in loads[3:]:
                local.wait()
        if i >= 5:
            next(first)
            next(first)
    pass_on(2)
    pass_on(3)
    next(first)
    next(first)

    back_order = [(0, 0), (0, 1), (1, 0), (1, 1), (0, 2), (0, 3), (1, 2), (1, 3)]

    def send_back(i):
        if i < len(back_order):
            rel, j = back_order[i]
            if rel:
                rim_return(j).wait_recv()
            cross_out(rel, j).start()

    def onto(i):
        cross_out(*back_order[i]).wait_send()
        send_back(i + WINDOW)
        cross_out(*back_order[i]).wait_recv()
        hop_out(*back_order[i]).start()

    send_back(0)
    send_back(1)
    next(first, None)
    send_back(2)
    second = waves(1)
    for i in range(5):
        next(second)
    onto(0)
    next(second)
    next(second)
    next(second)
    onto(1)
    onto(2)
    next(second, None)

    probe_swap().start()

    probe_swap().wait_recv()
    probe_part[2] = probe_part[depth] + probe_got[0]
    probe_step(0).start()

    done = 0
    for i in range(3, len(back_order)):
        onto(i)
        if i >= 5 and done < len(bits) - 1:
            probe_step(done).wait_recv()
            probe_part[3 + done] = probe_part[2 + done] + probe_got[1 + done]
            done += 1
            probe_step(done).start()
    while done < len(bits):
        probe_step(done).wait_recv()
        probe_part[3 + done] = probe_part[2 + done] + probe_got[1 + done]
        done += 1
        if done < len(bits):
            probe_step(done).start()
    probe_out[...] = probe_part[2 + len(bits)]
    own_k_out[...] = own_grad[0]

    def drain(j, carry):
        own_return(j).wait_recv()
        for rel in range(2):
            hop_out(rel, j).wait_recv()
            hop_out(rel, j).wait_send()
            cross_in(rel, j).wait_send()
        own_swap(j).wait_send()
        rim_swap(j).wait_send()
        own_return(j).wait_send()
        rim_return(j).wait_send()
        return carry

    lax.fori_loop(0, rounds, drain, 0)
    probe_swap().wait_send()
    for i in range(len(bits)):
        probe_step(i).wait_send()


def scatter_kernel(own_cols, near_place, far_place, own_k, own_g, near_k, near_g, far_k, far_g, out):
    depth, tile, odd = axis_places()
    blocks = out.shape[2] // LANES
    shape = (out.shape[0], out.shape[1], LANES)
    lane = lax.broadcasted_iota(jnp.int32, shape, 2)
    row = lax.broadcasted_iota(jnp.int32, shape, 1)
    out[...] = jnp.zeros_like(out)
    for index, ref in enumerate((own_k, own_g, near_k, near_g, far_k, far_g)):
        which, rel = index // 2, index % 2

        def one(j, carry, which=which, rel=rel, ref=ref):
            slot = 2 * j + (depth if rel == 0 else 1 - depth)
            value = ref[j]
            col = own_cols[slot] if which == 0 else (near_place, far_place)[which - 1][1, slot]
            if which:
                under = odd if which == 1 else 1 - odd
                place = (near_place, far_place)[which - 1]
                owner = tile + (1 - 2 * odd if which == 1 else 2 * odd - 1)
                start = place[0, slot] - (owner - 1) * shape[1]
                low = jnp.where(under == 1, 0, start)
                high = jnp.where(under == 1, start, shape[1])
                exists = (owner >= 0) & (owner < lax.axis_size("tile"))
                high = jnp.where(exists, high, low)
                value = jnp.where((row >= low) & (row < high), value, 0.0)
            block = col // LANES
            after = jnp.minimum(block + 1, blocks - 1)
            inside = lane >= col - block * LANES
            at = pl.ds(pl.multiple_of(block * LANES, LANES), LANES)
            out[:, :, at] = out[:, :, at] + jnp.where(inside, value, 0.0)
            at = pl.ds(pl.multiple_of(after * LANES, LANES), LANES)
            out[:, :, at] = out[:, :, at] + jnp.where(inside, 0.0, value)
            return carry

        lax.fori_loop(0, ref.shape[0], one, 0)


SMEM = pl.BlockSpec(memory_space=pltpu.SMEM)
VMEM = pl.BlockSpec(memory_space=pltpu.VMEM)
ANY = pl.BlockSpec(memory_space=pl.ANY)
PARAMS = pltpu.CompilerParams(vmem_limit_bytes=16 * 1024 * 1024)


def shards(transmission, probe, scan_rows, scan_cols, tile_counts, diffraction):
    size = probe.shape[-1]
    half = size // 2
    group, strip, cols = transmission.shape[1:]
    rounds = scan_rows.shape[0] // 2
    tiles = lax.axis_size("tile")
    f32 = jnp.float32

    beside = [(c, c ^ 1) for c in range(tiles)]
    across = [(c, c + 1 if c % 2 else c - 1) for c in range(1, tiles - 1)]

    place = jnp.stack([scan_rows, scan_cols])
    place_near = lax.ppermute(place, "tile", beside)
    place_far = lax.ppermute(place, "tile", across)

    flat = transmission.reshape(2 * group, strip, cols)
    piece = jax.ShapeDtypeStruct((rounds, 2 * group, strip, LANES), f32)
    own_k, own_g, near_k, near_g, far_k, far_g = pl.pallas_call(
        gather_kernel,
        out_shape=[piece] * 6,
        in_specs=[SMEM] * 3 + [VMEM],
        out_specs=[VMEM] * 6,
        compiler_params=PARAMS,
        name="gather",
    )(scan_cols, place_near, place_far, flat)

    tabs = [jnp.asarray(t) for t in tables(size)]
    pair = 2
    stages = (tiles - 1).bit_length()
    sems = pltpu.SemaphoreType.DMA((12 * rounds + 1 + stages,))
    both = pltpu.VMEM((2,) + piece.shape, f32)
    single = pltpu.VMEM(piece.shape, f32)
    waves = pltpu.VMEM((2 * group, 2, pair * size, size), f32)
    rows_shape = (probe.shape[0], half, size)
    *parts, probe_grad = pl.pallas_call(
        main_kernel,
        out_shape=[piece] * 6 + [jax.ShapeDtypeStruct(rows_shape, f32)],
        in_specs=[SMEM] * 4 + [ANY] * 12,
        out_specs=[VMEM] * 7,
        scratch_shapes=[both, both, both, single, single, both, both, both, both]
        + [waves, waves, pltpu.VMEM((2, pair * size, size), f32)]
        + [pltpu.VMEM((3 + stages,) + rows_shape, f32), pltpu.VMEM((1 + stages,) + rows_shape, f32)]
        + [pltpu.VMEM(probe.shape, f32), pltpu.VMEM(diffraction.shape, f32)]
        + [pltpu.VMEM(t.shape, t.dtype) for t in tabs]
        + [sems, sems, pltpu.SemaphoreType.DMA((9,))],
        compiler_params=pltpu.CompilerParams(
            vmem_limit_bytes=24 * 1024 * 1024, collective_id=0, has_side_effects=True
        ),
        name="waves",
    )(
        scan_rows, scan_cols, tile_counts, place_near, probe, diffraction,
        own_k, own_g, near_k, near_g, far_k, far_g, *tabs,
    )

    grads = pl.pallas_call(
        scatter_kernel,
        out_shape=jax.ShapeDtypeStruct(flat.shape, f32),
        in_specs=[SMEM] * 3 + [VMEM] * 6,
        out_specs=VMEM,
        compiler_params=PARAMS,
        name="scatter",
    )(scan_cols, place_near, place_far, *parts)
    return (grads.reshape(transmission.shape), probe_grad)


def solution(mesh):
    placed = (P(None, "depth", "tile", None), P(), P("tile"), P("tile"), P(), P("tile", None, None))
    return jax.shard_map(
        shards,
        mesh=mesh,
        in_specs=placed,
        out_specs=(P(None, "depth", "tile", None), P(None, "depth", None)),
        check_vma=False,
    )
```
